32 devices in a mesh: chan: 8 (over y, x, core), tm: 4 (over z).
Axes of the slice: x: 2, y: 2, z: 4, core: 2. Of those that a mesh axis runs over, the one named last changes fastest.
Arguments:
- voltages: bfloat16 [2, 2048, 131072], P(None, 'chan', 'tm'), may hold values from -6 to 6
- filter_taps: float32 [16, 64], replicated, may hold values from -1.5 to 1.5
- antenna_flags: int32 [2048], P('chan'), may hold values 0 or 1
Outputs:
- visibility: float32 [2048, 2, 8, 2048], P('tm', None, 'chan')
The draws below stay inside these ranges and needn't reach their ends.
All inputs are finite; a program needn't handle non-finite values. No bound on the sum of `antenna_flags` on one device may be relied on, other than what follows from the above.
Results may differ from the reference program's by a relative error of at most 0.0028.
Values may be sent and summed in bfloat16 or wider, within the bound.
No kernel may reach another device: no remote copies, remote signals or barrier semaphores. Data moves between devices by JAX's collectives and lax.ppermute only.
A program may use at most 320 MiB of HBM per device.

```python
import math
import jax
import jax.numpy as jnp
from jax import lax

A = 2048
NFFT = 64
TAPS = 16
CH = 8
FRAMES = 2048
SAMPLES = 131072


def set_ends(array, own_key, least, top_value):
    shape = array.shape
    spot = [jax.random.randint(jax.random.fold_in(own_key, axis), (), 0, shape[axis]) for axis in range(len(shape))]
    array = array.at[tuple(spot)].set(least)
    longest = shape.index(max(shape))
    spot[longest] = (spot[longest] + 1) % shape[longest]
    return array.at[tuple(spot)].set(top_value)


def block_levels(key, extent, shards, low, largest):
    factor_of, own = 1.0, jax.random.fold_in(key, 6)
    for axis_at, blocks in shards:
        heights = jnp.exp(jax.random.uniform(jax.random.fold_in(own, axis_at), (blocks,), jnp.float32, low / len(shards), largest / len(shards)))
        factor_of = factor_of * jnp.repeat(heights, extent[axis_at] // blocks).reshape([-1 if axis == axis_at else 1 for axis in range(len(extent))])
    return factor_of


def noise(key, dims, deviation, most, split=(), held_as=jnp.bfloat16):
    array = jax.random.normal(key, dims, jnp.float32) * deviation
    if len(split) > 0:
        array = block_levels(key, dims, split, -0.22, 0.18) * array
    return jnp.clip(array, min=-most, max=most).astype(held_as)


def setup_inputs(seed: int = 0) -> dict:
    key_list = jax.random.split(jax.random.key(seed), 4)
    voltages = noise(key_list[0], (2, A, SAMPLES), 1.0, 6.0, ((1, 8), (2, 4)))
    filter_taps = noise(key_list[1], (TAPS, NFFT), 0.25, 1.5, (), jnp.float32)
    antenna_flags = set_ends((jax.random.randint(key_list[2], (A,), 0, 8) < 7).astype(jnp.int32), jax.random.fold_in(key_list[2], 1), 0, 1)
    return dict(voltages=voltages, filter_taps=filter_taps, antenna_flags=antenna_flags)


def dft_tables(signal_length, count):
    index_n = jnp.arange(signal_length, dtype=jnp.int32)
    index_c = jnp.arange(count, dtype=jnp.int32)
    phase = index_n[:, None] * index_c[None, :] % signal_length
    angle = phase.astype(jnp.float32) * (2.0 * math.pi / signal_length)
    return (jnp.cos(angle), jnp.sin(angle))

def spectra_one(signal, filter_taps, flag, cosine, sine_table):
    frames = signal.astype(jnp.float32).reshape(2, FRAMES, NFFT)
    padded = jnp.concatenate([jnp.zeros((2, TAPS - 1, NFFT), jnp.float32), frames], axis=1)
    filter_output = jnp.zeros((2, FRAMES, NFFT), jnp.float32)
    for tap_index in range(TAPS):
        begin = TAPS - 1 - tap_index
        filter_output = filter_output + filter_taps[tap_index][None, None, :] * padded[:, begin:begin + FRAMES, :]
    cos_part = jnp.einsum('pfn,nc->pcf', filter_output, cosine, precision=lax.Precision.HIGHEST)
    sin_part = jnp.einsum('pfn,nc->pcf', filter_output, sine_table, precision=lax.Precision.HIGHEST)
    scale = flag.astype(jnp.float32) / math.sqrt(NFFT)
    real_part = (cos_part[0] + sin_part[1]) * scale
    imag_part = (cos_part[1] - sin_part[0]) * scale
    return jnp.stack([real_part, imag_part]).astype(jnp.bfloat16)

def one_channel(pair):
    real_part = pair[0]
    imag_part = pair[1]
    high = lax.Precision.HIGHEST
    visibility_real = jnp.dot(real_part, real_part.T, precision=high) + jnp.dot(imag_part, imag_part.T, precision=high)
    visibility_imaginary = jnp.dot(imag_part, real_part.T, precision=high) - jnp.dot(real_part, imag_part.T, precision=high)
    return jnp.stack([visibility_real, visibility_imaginary]) / FRAMES

def reference(voltages, filter_taps, antenna_flags):
    cosine, sine_table = dft_tables(NFFT, CH)
    per_antenna = jnp.transpose(voltages, (1, 0, 2))
    spectra = lax.map(lambda item: spectra_one(item[0], filter_taps, item[1], cosine, sine_table), (per_antenna, antenna_flags))
    spectra = jnp.transpose(spectra, (2, 1, 0, 3)).astype(jnp.float32)
    result = lax.map(one_channel, spectra)
    return jnp.transpose(result, (2, 1, 0, 3))
```

```python
import functools
import math

import jax
import jax.numpy as jnp
import numpy as np
from jax import lax
from jax.experimental import pallas as pl
from jax.experimental.pallas import tpu as pltpu
from jax.sharding import PartitionSpec as P

F32, BF16 = jnp.float32, jnp.bfloat16
GROUP = 8
VMEM_LIMIT = 48 * 1024 * 1024


def params(**more):
    return pltpu.CompilerParams(vmem_limit_bytes=VMEM_LIMIT, **more)


def filterbank_weights(filter_taps, channels):
    taps, length = filter_taps.shape
    phase = np.arange(length)[None, :] * np.arange(channels)[:, None] % length
    angle = phase * (2.0 * math.pi / length)
    trig = np.stack([np.cos(angle), np.sin(angle)]).reshape(2 * channels, length)
    trig = np.tile(trig, (1, taps)).astype(np.float32)
    base = filter_taps[::-1].reshape(1, taps * length) * trig
    wide = (taps + GROUP) * length
    rows = [
        jnp.pad(base, ((0, 0), ((f + 1) * length, wide - (f + 1 + taps) * length)))
        for f in range(GROUP)
    ]
    weights = jnp.stack(rows, axis=1).reshape(2 * channels * GROUP, wide)
    high = lax.reduce_precision(weights, 8, 7)
    return jnp.concatenate([high, weights - high], axis=0).astype(BF16)


def filterbank_kernel(channels, length, head_ref, v_ref, w_ref, s_ref, out_ref, window):
    step = pl.program_id(0)
    _, part, lanes = v_ref.shape
    head = head_ref.shape[2]
    wide = w_ref.shape[1]

    @pl.when(step == 0)
    def _():
        window[:, :head] = head_ref[...].reshape(2 * part, head)

    @pl.when(step > 0)
    def _():
        window[:, :head] = window[:, lanes:]

    window[:, head:] = v_ref[...].reshape(2 * part, lanes)
    scale = s_ref[...]
    half = channels * GROUP
    groups = lanes // (length * GROUP)

    def one(g):
        x = window[:, g * GROUP * length : g * GROUP * length + wide]
        r = lax.dot_general(w_ref[...], x, (((1,), (1,)), ((), ())), preferred_element_type=F32)
        r = r[: 2 * half] + r[2 * half :]
        cos, sin = r[:half], r[half:]
        real = (cos[:, :part] + sin[:, part:]) * scale
        imag = (cos[:, part:] - sin[:, :part]) * scale
        return real, imag

    for g in range(0, groups, 2):
        first, second = one(g), one(g + 1)
        for c in range(channels):
            rows = slice(c * GROUP, (c + 1) * GROUP)
            for ri in range(2):
                both = jnp.concatenate([first[ri][rows], second[ri][rows]], axis=0)
                out_ref[c, ri, g * GROUP : (g + 2) * GROUP, :] = both.astype(BF16)


def filterbank(voltages, halo, weights, scale, length, channels, part, h, t, frames):
    block = min(frames, 32)
    lanes = block * length
    head = halo.shape[2]
    first = t * frames * length
    if t == 0:
        before, head_map = halo, lambda s: (0, h, 0)
    else:
        before, head_map = voltages, lambda s: (0, h, first // head - 1)
    return pl.pallas_call(
        functools.partial(filterbank_kernel, channels, length),
        grid=(frames // block,),
        in_specs=[
            pl.BlockSpec((2, part, head), head_map),
            pl.BlockSpec((2, part, lanes), lambda s: (0, h, first // lanes + s)),
            pl.BlockSpec(weights.shape, lambda s: (0, 0)),
            pl.BlockSpec((1, part), lambda s: (0, h)),
        ],
        out_specs=pl.BlockSpec((channels, 2, block, part), lambda s: (0, 0, s, 0)),
        out_shape=jax.ShapeDtypeStruct((channels, 2, frames, part), BF16),
        scratch_shapes=[pltpu.VMEM((2 * part, head + lanes), BF16)],
        compiler_params=params(),
        cost_estimate=pl.CostEstimate(
            flops=2 * weights.size * 2 * part * frames // GROUP,
            bytes_accessed=2 * 2 * part * frames * length,
            transcendentals=0,
        ),
        name=f"filterbank_h{h}_t{t}",
    )(before, voltages, weights, scale)


def correlate_kernel(times, span, weight, fresh, same, tab, *refs):
    xs, ys = refs[:times], refs[times : 2 * times]
    out_ref = refs[2 * times] if fresh else refs[2 * times + 1]
    pair = pl.program_id(0)
    i, j = tab[0, pair], tab[1, pair]

    def side(ref, at, ri):
        return jnp.concatenate([ref[at * span + d, ri] for d in range(span)], axis=1)

    def product(x, y):
        return lax.dot_general(x, y, (((0,), (0,)), ((), ())), preferred_element_type=F32)

    real = imag = None
    for x_ref, y_ref in zip(xs, ys):
        xr, xi = side(x_ref, i, 0), side(x_ref, i, 1)
        yr, yi = side(y_ref, j, 0), side(y_ref, j, 1)
        re = product(xr, yr) + product(xi, yi)
        im = product(xi, yr) - product(xr, yi)
        real = re if real is None else real + re
        imag = im if imag is None else imag + im
    real, imag = real * weight, imag * weight
    if not same:
        out_ref[0] = real
        out_ref[1] = imag
        return

    @pl.when(i != j)
    def _():
        out_ref[0] = real
        out_ref[1] = imag

    @pl.when(i == j)
    def _():
        row = lax.broadcasted_iota(jnp.int32, real.shape, 0)
        col = lax.broadcasted_iota(jnp.int32, real.shape, 1)
        out_ref[0] = jnp.where(row >= col, real, imag)


def correlate(partial, total, pairs, first, xs, ys, span, weight, same):
    times = len(xs)
    size = span * xs[0].shape[3]
    table = np.asarray(pairs, np.int32).T
    whole = [pl.BlockSpec(a.shape, lambda p, tab: (0, 0, 0, 0)) for a in xs + ys]
    out_block = pl.BlockSpec((2, size, size), lambda p, tab: (first + p, 0, 0))
    shape = jax.ShapeDtypeStruct((total, size, size), F32)
    store = jax.ShapeDtypeStruct((total, size, size), BF16)
    fresh = partial is None
    anywhere = pl.BlockSpec(memory_space=pl.ANY)
    return pl.pallas_call(
        functools.partial(correlate_kernel, times, span, weight, fresh, same),
        grid_spec=pltpu.PrefetchScalarGridSpec(
            num_scalar_prefetch=1,
            grid=(len(pairs),),
            in_specs=whole + ([] if fresh else [anywhere]),
            out_specs=[out_block, anywhere, anywhere] if fresh else [out_block],
        ),
        out_shape=[shape, store, store] if fresh else [shape],
        input_output_aliases={} if fresh else {1 + 2 * times: 0},
        compiler_params=params(),
        cost_estimate=pl.CostEstimate(
            flops=len(pairs) * 8 * size * size * times * xs[0].shape[2],
            bytes_accessed=len(pairs) * 8 * size * size,
            transcendentals=0,
        ),
        name="correlate",
    )(jnp.asarray(table), *xs, *ys, *([] if fresh else [partial]))


class Plan:
    def __init__(self, slices, parts, count):
        self.slices, self.parts, self.count = slices, parts, count
        self.calls = []
        self.pair_at = {}
        for h in range(parts):
            for k in range(h, -1, -1):
                pairs = [
                    (i, j) for i in range(slices) for j in range(slices) if k < h or j <= i
                ]
                self.calls.append((h, k, pairs, len(self.pair_at)))
                for i, j in pairs:
                    self.pair_at[h, i, k, j] = len(self.pair_at)
        self.spare = 2 * len(self.pair_at)
        self.total = self.spare + 2
        self.right = self.messages(lambda i, j: max(i, j))
        self.left = self.messages(lambda i, j: slices - 1 - min(i, j))
        self.steps = 0
        for index in range(2 * (len(self.right) + len(self.left)) + 4 * slices):
            if self.senders(self.right, index) or self.senders(self.left, index):
                self.steps = index + 1

    def squares(self, h, i, k, j):
        at = 2 * self.pair_at[h, i, k, j]
        return (at, at) if (h, i) == (k, j) else (at, at + 1)

    def messages(self, reach):
        queues, last = [[] for _ in range(self.parts)], []
        for (h, i, k, j) in self.pair_at:
            far = reach(i, j)
            if far:
                for square in sorted(set(self.squares(h, i, k, j))):
                    (queues[h] if far > 1 else last).append((-far, square))
        if self.slices == 2:
            queues, last = [sorted(last)], []
        found = []
        for queue in [sorted(q) for q in queues] + [sorted(last)]:
            for at in range(0, len(queue), self.count):
                some = queue[at : at + self.count]
                ids = [square for _, square in some]
                ids += [self.spare] * (self.count - len(ids))
                found.append((ids, max(-far for far, _ in some)))
        return found

    def senders(self, messages, step):
        places = []
        for place in range(self.slices - 1):
            k = step - 2 * place
            if 0 <= k < len(messages) and messages[k][1] > place:
                places.append(place)
        return places

    def table(self):
        rows = np.full((self.slices, self.steps + 2, 2 * self.count), self.spare, np.int32)
        for z in range(self.slices):
            for step in range(self.steps + 2):
                for side, (messages, place) in enumerate(
                    ((self.right, z), (self.left, self.slices - 1 - z))
                ):
                    k = step - 2 * place
                    if 0 <= k < len(messages):
                        rows[z, step, side * self.count : (side + 1) * self.count] = messages[k][0]
        return rows

    def last_part(self, step):
        need = 0
        for messages in (self.right, self.left):
            for place in range(self.slices):
                k = step - 2 * place
                if 0 <= k < len(messages):
                    for square in messages[k][0]:
                        for (h, i, c, j), at in self.pair_at.items():
                            if at == square // 2:
                                need = max(need, h)
        return need

    def outputs(self):
        z_n, h_n = self.slices, self.parts
        ids = np.zeros((z_n, h_n, z_n, h_n, 2), np.int32)
        modes = np.zeros((z_n, h_n, z_n, h_n), np.int32)
        for z in range(z_n):
            for h in range(h_n):
                for j in range(z_n):
                    for k in range(h_n):
                        if (h, z, k, j) in self.pair_at:
                            ids[z, h, j, k] = self.squares(h, z, k, j)
                            modes[z, h, j, k] = 2 if (h, z) == (k, j) else 0
                        else:
                            ids[z, h, j, k] = self.squares(k, j, h, z)
                            modes[z, h, j, k] = 1
        return ids, modes


def hop_kernel(receives, sends, tab, *refs):
    refs = list(refs)
    p_right, p_left = refs[0], refs[1]
    at = 2
    if receives:
        in_right, in_left = refs[2], refs[3]
        at = 6
    outs = refs[at:]
    if receives:
        keep_right, keep_left = outs[0], outs[1]
        outs = outs[2:]
        keep_right[...] = in_right[...]
        keep_left[...] = in_left[...]
        if sends:
            outs[0][...] = (p_right[...] + in_right[...].astype(F32)).astype(BF16)
            outs[1][...] = (p_left[...] + in_left[...].astype(F32)).astype(BF16)
    else:
        outs[0][...] = p_right[...].astype(BF16)
        outs[1][...] = p_left[...].astype(BF16)


def hop(table, step, count, partial, received, kept, sends):
    size = partial.shape[1]
    block = (1, size, size)
    right = pl.BlockSpec(block, lambda b, tab: (tab[step, b], 0, 0))
    left = pl.BlockSpec(block, lambda b, tab: (tab[step, count + b], 0, 0))
    plain = pl.BlockSpec(block, lambda b, tab: (b, 0, 0))
    anywhere = pl.BlockSpec(memory_space=pl.ANY)
    receives = received is not None
    message = jax.ShapeDtypeStruct((count, size, size), BF16)
    in_specs, operands = [right, left], [partial, partial]
    out_specs, out_shape, aliases = [], [], {}
    if receives:
        in_specs += [plain, plain, anywhere, anywhere]
        operands += [*received, *kept]
        out_specs += [right, left]
        out_shape += [jax.ShapeDtypeStruct(k.shape, k.dtype) for k in kept]
        aliases = {5: 0, 6: 1}
    if sends:
        out_specs += [plain, plain]
        out_shape += [message, message]
    found = pl.pallas_call(
        functools.partial(hop_kernel, receives, sends),
        grid_spec=pltpu.PrefetchScalarGridSpec(
            num_scalar_prefetch=1, grid=(count,), in_specs=in_specs, out_specs=out_specs
        ),
        out_shape=out_shape,
        input_output_aliases=aliases,
        compiler_params=params(),
        cost_estimate=pl.CostEstimate(
            flops=4 * count * size * size, bytes_accessed=20 * count * size * size, transcendentals=0
        ),
        name="hop",
    )(table, *operands)
    if receives:
        kept, found = found[:2], found[2:]
    return kept, (found if sends else None)


def rows_kernel(slices, parts, span, part, stride, local, tab, mode, ends, *refs):
    n = slices * parts * 2
    own, right, left = refs[:n], refs[n : 2 * n], refs[2 * n : 3 * n]
    out_ref = refs[3 * n]
    h, d = pl.program_id(0), pl.program_id(1)
    has_right, has_left = ends[0] > 0, ends[1] > 0
    size = span * part
    rows = pl.ds(pl.multiple_of(d * part, part), part)

    def plain(at):
        r = jnp.where(has_right, right[at][0, rows, :].astype(F32), 0.0)
        l = jnp.where(has_left, left[at][0, rows, :].astype(F32), 0.0)
        return own[at][0, rows, :] + r + l

    def turned(at):
        r = jnp.where(has_right, right[at][0, :, rows].astype(F32), 0.0)
        l = jnp.where(has_left, left[at][0, :, rows].astype(F32), 0.0)
        return (own[at][0, :, rows] + r + l).T

    for j in range(slices):
        for k in range(parts):
            at = 2 * (j * parts + k)
            kind = mode[(h * slices + j) * parts + k]

            def put(ri, value, j=j, k=k):
                for e in range(span):
                    tile = ((j * span + e) * local + k * part) // 128
                    out_ref[pl.ds(ri * (stride // 2) + tile, part, stride=stride), :] = value[
                        :, e * part : (e + 1) * part
                    ]

            @pl.when(kind == 0)
            def _():
                put(0, plain(at))
                put(1, plain(at + 1))

            @pl.when(kind == 1)
            def _():
                put(0, turned(at))
                put(1, -turned(at + 1))

            @pl.when(kind == 2)
            def _():
                direct, mirror = plain(at), turned(at)
                row = lax.broadcasted_iota(jnp.int32, (part, size), 0) + d * part
                col = lax.broadcasted_iota(jnp.int32, (part, size), 1)
                put(0, jnp.where(row >= col, direct, mirror))
                put(1, jnp.where(row < col, direct, jnp.where(row == col, 0.0, -mirror)))


def visibility_rows(plan, partial, kept, span, part, antennas):
    slices, parts = plan.slices, plan.parts
    size = span * part
    local = parts * part
    ids, modes = plan.outputs()
    z = lax.axis_index("tm")
    table = jnp.asarray(ids.reshape(slices, -1))[z]
    mode = jnp.asarray(modes.reshape(slices, -1))[z]
    ends = jnp.stack([z, slices - 1 - z]).astype(jnp.int32)
    per_h = slices * parts * 2

    def spec(at):
        return pl.BlockSpec(
            (1, size, size), lambda h, d, tab, mode, ends: (tab[h * per_h + at], 0, 0)
        )

    stride = 2 * antennas // 128
    out = pl.pallas_call(
        functools.partial(rows_kernel, slices, parts, span, part, stride, local),
        grid_spec=pltpu.PrefetchScalarGridSpec(
            num_scalar_prefetch=3,
            grid=(parts, span),
            in_specs=[spec(at) for _ in range(3) for at in range(per_h)],
            out_specs=pl.BlockSpec(
                (part * stride, 128), lambda h, d, tab, mode, ends: (d * parts + h, 0)
            ),
        ),
        out_shape=jax.ShapeDtypeStruct((span * local * stride, 128), F32),
        compiler_params=params(),
        name="visibility_rows",
    )(table, mode, ends, *([partial] * per_h), *([kept[0]] * per_h), *([kept[1]] * per_h))
    return out.reshape(span * local, 2, 1, antennas)


def on_device(voltages, filter_taps, antenna_flags):
    taps, length = filter_taps.shape
    channels, slices = lax.axis_size("chan"), lax.axis_size("tm")
    local = voltages.shape[1]
    samples = voltages.shape[2]
    frames = samples // length
    part = 128
    parts = local // part
    span = channels // slices
    times = 2
    chunk = frames // times

    head = taps * length
    tail = voltages[:, :, samples - head :]
    halo = lax.ppermute(tail, "tm", [(i, i + 1) for i in range(slices - 1)])
    weights = filterbank_weights(filter_taps, channels)
    scale = (antenna_flags.astype(F32) / math.sqrt(length)).reshape(1, local)

    spectra = []
    for h in range(parts):
        found = {}
        for t in reversed(range(times)):
            own = filterbank(
                voltages, halo, weights, scale, length, channels, part, h, t, chunk
            )
            found[t] = lax.all_to_all(own, "chan", split_axis=0, concat_axis=0, tiled=True)
        spectra.append([found[t] for t in range(times)])

    plan = Plan(slices, parts, 4)
    table = jnp.asarray(plan.table())[lax.axis_index("tm")]
    weight = 1.0 / (frames * slices)
    partial, kept = None, None
    calls = list(plan.calls)

    def extend(partial, kept, upto):
        while calls and calls[0][0] <= upto:
            h, k, pairs, first = calls.pop(0)
            made = correlate(
                partial, plan.total, pairs, first, spectra[h], spectra[k], span, weight, h == k
            )
            partial = made[0]
            if kept is None:
                kept = made[1:]
        return partial, kept

    arrived = {}
    for step in range(plan.steps + 2):
        partial, kept = extend(partial, kept, plan.last_part(step))
        sends = step < plan.steps
        received = arrived.pop(step - 2, None)
        kept, outgoing = hop(table, step, plan.count, partial, received, kept, sends)
        if sends:
            right = [(p, p + 1) for p in plan.senders(plan.right, step)]
            end = slices - 1
            left = [(end - p, end - p - 1) for p in plan.senders(plan.left, step)]
            arrived[step] = [
                lax.ppermute(outgoing[0], "tm", right),
                lax.ppermute(outgoing[1], "tm", left),
            ]
    partial, kept = extend(partial, kept, parts)
    return visibility_rows(plan, partial, kept, span, part, channels * local)


def solution(mesh):
    placed = (P(None, "chan", "tm"), P(), P("chan"))
    return jax.shard_map(
        on_device,
        mesh=mesh,
        in_specs=placed,
        out_specs=P("tm", None, "chan", None),
        check_vma=False,
    )
```

```python
import functools
import math

import jax
import jax.numpy as jnp
import numpy as np
from jax import lax
from jax.experimental import pallas as pl
from jax.experimental.pallas import tpu as pltpu
from jax.sharding import PartitionSpec as P

F32, BF16 = jnp.float32, jnp.bfloat16
GROUP = 8
LANES = 128
VMEM_LIMIT = 52 * 1024 * 1024


def params(limit=VMEM_LIMIT):
    return pltpu.CompilerParams(vmem_limit_bytes=limit)


def weights_kernel(taps_ref, trig_ref, out_ref, wide):
    taps, length = taps_ref.shape
    rows = trig_ref.shape[0]
    size = GROUP * length
    flat = jnp.concatenate([taps_ref[taps - 1 - k : taps - k, :] for k in range(taps)], axis=1)
    base = flat * jnp.concatenate([trig_ref[...]] * taps, axis=1)
    for f in range(GROUP):
        before = jnp.zeros((rows, (f + 1) * length), F32)
        moved = [before, base]
        if f < GROUP - 1:
            moved.append(jnp.zeros((rows, (GROUP - 1 - f) * length), F32))
        moved = jnp.concatenate(moved, axis=1)
        for t in range(wide.shape[0]):
            wide[t, pl.ds(f, rows, stride=GROUP), :] = moved[:, t * LANES : (t + 1) * LANES]
    n = rows * GROUP
    each = size // LANES
    for t in range(wide.shape[0]):
        full = wide[t]
        high = full.astype(BF16)
        low = (full - high.astype(F32)).astype(BF16)
        m, lanes = t // each, slice(t % each * LANES, (t % each + 1) * LANES)
        out_ref[2 * m * n : (2 * m + 1) * n, lanes] = high
        out_ref[(2 * m + 1) * n : (2 * m + 2) * n, lanes] = low


def filterbank_weights(filter_taps, channels):
    taps, length = filter_taps.shape
    phase = np.arange(length)[None, :] * np.arange(channels)[:, None] % length
    angle = phase * (2.0 * math.pi / length)
    trig = np.stack([np.cos(angle), np.sin(angle)]).reshape(2 * channels, length)
    rows = 2 * channels * GROUP
    blocks = taps // GROUP + 1
    return pl.pallas_call(
        weights_kernel,
        out_shape=jax.ShapeDtypeStruct((blocks * 2 * rows, GROUP * length), BF16),
        scratch_shapes=[pltpu.VMEM((blocks * GROUP * length // LANES, rows, LANES), F32)],
        compiler_params=params(),
        name="weights",
    )(filter_taps, jnp.asarray(trig.astype(np.float32)))


def filterbank_kernel(channels, length, head_ref, v_ref, w_ref, s_ref, after_ref, out_ref, token_ref, carry):
    del after_ref, token_ref
    step = pl.program_id(0)
    _, part, lanes = v_ref.shape
    size = GROUP * length
    half = channels * GROUP
    rows = 2 * half
    blocks = w_ref.shape[0] // (2 * rows)
    scale = s_ref[...]

    def advance(ref, at):
        x = ref[:, :, at * size : (at + 1) * size].reshape(2 * part, size)
        r = lax.dot_general(w_ref[...], x, (((1,), (1,)), ((), ())), preferred_element_type=F32)
        third = [
            r[2 * m * rows : (2 * m + 1) * rows] + r[(2 * m + 1) * rows : (2 * m + 2) * rows]
            for m in range(blocks)
        ]
        done = carry[blocks - 2] + third[blocks - 1]
        for m in range(blocks - 2, 0, -1):
            carry[m] = carry[m - 1] + third[m]
        carry[0] = third[0]
        return done

    @pl.when(step == 0)
    def _():
        carry[...] = jnp.zeros_like(carry)
        for b in range(head_ref.shape[2] // size):
            advance(head_ref, b)

    def one(b):
        done = advance(v_ref, b)
        cos, sin = done[:half], done[half:]
        real = (cos[:, :part] + sin[:, part:]) * scale
        imag = (cos[:, part:] - sin[:, :part]) * scale
        return real, imag

    for b in range(0, lanes // size, 2):
        first, second = one(b), one(b + 1)
        for c in range(channels):
            take = slice(c * GROUP, (c + 1) * GROUP)
            for ri in range(2):
                both = jnp.concatenate([first[ri][take], second[ri][take]], axis=0)
                out_ref[c, ri, b * GROUP : (b + 2) * GROUP, :] = both.astype(BF16)


def filterbank(voltages, halo, weights, scale, length, channels, part, h, start, frames, after):
    block = min(frames, 64)
    lanes = block * length
    head = halo.shape[2]
    first = start * length
    if start == 0:
        before, head_map = halo, lambda s: (0, 0, 0)
    else:
        before, head_map = voltages, lambda s: (0, h, first // head - 1)
    blocks = head // (GROUP * length)
    return pl.pallas_call(
        functools.partial(filterbank_kernel, channels, length),
        grid=(frames // block,),
        in_specs=[
            pl.BlockSpec((2, part, head), head_map),
            pl.BlockSpec((2, part, lanes), lambda s: (0, h, first // lanes + s)),
            pl.BlockSpec(weights.shape, lambda s: (0, 0)),
            pl.BlockSpec((1, part), lambda s: (0, h)),
            pl.BlockSpec(memory_space=pl.ANY),
        ],
        out_specs=[
            pl.BlockSpec((channels, 2, block, part), lambda s: (0, 0, s, 0)),
            pl.BlockSpec(memory_space=pl.ANY),
        ],
        out_shape=[
            jax.ShapeDtypeStruct((channels, 2, frames, part), BF16),
            jax.ShapeDtypeStruct((8, LANES), F32),
        ],
        scratch_shapes=[pltpu.VMEM((blocks, 2 * channels * GROUP, 2 * part), F32)],
        compiler_params=params(),
        cost_estimate=pl.CostEstimate(
            flops=2 * weights.size * 2 * part * frames // GROUP,
            bytes_accessed=2 * 2 * part * frames * length,
            transcendentals=0,
        ),
        name=f"filterbank_h{h}_f{start}",
    )(before, voltages, weights, scale, after)


def correlate_kernel(nx, ny, span, weight, fresh, same, low, *refs):
    xs = refs[:nx]
    ys = xs if same else refs[nx : nx + ny]
    at = nx if same else nx + ny
    out_ref = refs[at] if fresh else refs[at + 1]
    i = pl.program_id(0) + low
    part = xs[0].shape[3]
    size = span * part
    count = ys[0].shape[0] // span

    def side(some, first, many, ri):
        wide = [
            jnp.concatenate([ref[first + d, ri] for d in range(many)], axis=1) for ref in some
        ]
        return wide[0] if len(wide) == 1 else jnp.concatenate(wide, axis=0)

    real, imag = side(xs, i * span, span, 0).T, side(xs, i * span, span, 1).T
    on_real = jnp.concatenate([real, imag], axis=0)
    on_imag = jnp.concatenate([imag, -real], axis=0)
    group = 2 if count % 2 == 0 else 1

    def columns_from(first):
        both = jnp.dot(on_real, side(ys, first * span, group * span, 0), preferred_element_type=F32)
        both = both + jnp.dot(
            on_imag, side(ys, first * span, group * span, 1), preferred_element_type=F32
        )
        both = both * weight
        for n in range(group):
            columns = slice(n * size, (n + 1) * size)
            out_ref[2 * (first + n)] = both[:size, columns]
            out_ref[2 * (first + n) + 1] = both[size:, columns]
            if same:

                @pl.when(i == first + n)
                def _():
                    row = lax.broadcasted_iota(jnp.int32, (size, size), 0)
                    col = lax.broadcasted_iota(jnp.int32, (size, size), 1)
                    out_ref[2 * (first + n)] = jnp.where(
                        row >= col, both[:size, columns], both[size:, columns]
                    )

    for first in range(0, count, group):
        if same and first > 0:
            pl.when(i >= first)(functools.partial(columns_from, first))
        else:
            columns_from(first)


def correlate(partial, total, slices, call, xs, ys, span, weight, same, low, high):
    size = span * xs[0].shape[3]
    frames = sum(x.shape[2] for x in xs)
    spectra = xs if same else xs + ys
    whole = [pl.BlockSpec(a.shape, lambda i: (0, 0, 0, 0)) for a in spectra]
    out_block = pl.BlockSpec((2 * slices, size, size), lambda i: (call * slices + low + i, 0, 0))
    shape = jax.ShapeDtypeStruct((total, size, size), F32)
    store = jax.ShapeDtypeStruct((total, size, size), BF16)
    fresh = partial is None
    anywhere = pl.BlockSpec(memory_space=pl.ANY)
    return pl.pallas_call(
        functools.partial(correlate_kernel, len(xs), len(ys), span, weight, fresh, same, low),
        grid=(high - low,),
        in_specs=whole + ([] if fresh else [anywhere]),
        out_specs=[out_block, anywhere, anywhere] if fresh else [out_block],
        out_shape=[shape, store, store] if fresh else [shape],
        input_output_aliases={} if fresh else {len(whole): 0},
        compiler_params=params(),
        cost_estimate=pl.CostEstimate(
            flops=8 * (high - low) * slices * size * size * frames,
            bytes_accessed=8 * (high - low) * slices * size * size,
            transcendentals=0,
        ),
        name="correlate",
    )(*spectra, *([] if fresh else [partial]))


class Plan:
    def __init__(self, slices, parts, count):
        self.slices, self.parts, self.count = slices, parts, count
        self.calls = []
        self.pair_at = {}
        for h in range(parts):
            for k in range(h, -1, -1):
                first = len(self.calls) * slices * slices
                self.calls.append((h, k))
                for i in range(slices):
                    for j in range(slices):
                        if k < h or j <= i:
                            self.pair_at[h, i, k, j] = first + i * slices + j
        self.spare = 2 * len(self.calls) * slices * slices
        self.total = self.spare + 2 * count
        self.right = self.messages(lambda i, j: max(i, j))
        self.left = self.messages(lambda i, j: slices - 1 - min(i, j))
        self.steps = 0
        for index in range(2 * (len(self.right) + len(self.left)) + 4 * slices):
            if self.senders(self.right, index) or self.senders(self.left, index):
                self.steps = index + 1

    def squares(self, h, i, k, j):
        at = 2 * self.pair_at[h, i, k, j]
        return (at, at) if (h, i) == (k, j) else (at, at + 1)

    def messages(self, reach):
        queues, last = [[] for _ in self.calls], []
        for (h, i, k, j) in self.pair_at:
            far = reach(i, j)
            if far:
                late = self.late(i, j) and self.late(j, i)
                for square in sorted(set(self.squares(h, i, k, j))):
                    (queues[self.call_of(h, k)] if far > 1 else last).append((-far, late, square))
        if self.slices == 2:
            queues, last = [last], []
        found = []
        for queue in [sorted(q) for q in queues] + [sorted(last)]:
            for at in range(0, len(queue), self.count):
                some = queue[at : at + self.count]
                ids = [square for _, _, square in some]
                found.append((ids, max(-far for far, _, _ in some)))
        return found

    def late(self, z, j):
        return (2 * z < self.slices) == (2 * j < self.slices)

    def first_ready(self):
        ready = 0
        ids, _ = self.outputs()
        for z in range(self.slices):
            for messages, place in ((self.right, z), (self.left, self.slices - 1 - z)):
                if place == 0:
                    continue
                for k, (squares, _) in enumerate(messages):
                    for j in range(self.slices):
                        if not self.late(z, j) and set(ids[z, :, j].ravel()) & set(squares):
                            ready = max(ready, k + 2 * place)
        return ready

    def senders(self, messages, step):
        places = []
        for place in range(self.slices - 1):
            k = step - 2 * place
            if 0 <= k < len(messages) and messages[k][1] > place:
                places.append(place)
        return places

    def table(self):
        rows = np.tile(
            self.spare + np.arange(2 * self.count, dtype=np.int32), (self.slices, self.steps + 2, 1)
        )
        for z in range(self.slices):
            for step in range(self.steps + 2):
                for side, (messages, place) in enumerate(
                    ((self.right, z), (self.left, self.slices - 1 - z))
                ):
                    k = step - 2 * place
                    if 0 <= k < len(messages):
                        for b, square in enumerate(messages[k][0]):
                            rows[z, step, side * self.count + b] = square
        return rows.reshape(-1)

    def call_of(self, h, k):
        return self.calls.index((h, k))

    def last_call(self, step):
        need = 0
        for messages in (self.right, self.left):
            for place in range(self.slices):
                k = step - 2 * place
                if 0 <= k < len(messages):
                    for square in messages[k][0]:
                        for (h, i, c, j), at in self.pair_at.items():
                            if at == square // 2:
                                need = max(need, self.call_of(h, c))
        return need

    def outputs(self):
        z_n, h_n = self.slices, self.parts
        ids = np.zeros((z_n, h_n, z_n, h_n, 2), np.int32)
        modes = np.zeros((z_n, h_n, z_n, h_n), np.int32)
        for z in range(z_n):
            for h in range(h_n):
                for j in range(z_n):
                    for k in range(h_n):
                        if (h, z, k, j) in self.pair_at:
                            ids[z, h, j, k] = self.squares(h, z, k, j)
                            modes[z, h, j, k] = 2 if (h, z) == (k, j) else 0
                        else:
                            ids[z, h, j, k] = self.squares(k, j, h, z)
                            modes[z, h, j, k] = 1
        return ids, modes


def hop_kernel(receives, sends, held, count, steps, step, tab, place, *refs):
    refs = list(refs)
    partial = refs.pop(0) if sends else None
    came = [refs.pop(0) for _ in range(2 if receives else 0)]
    outs = refs[held:]
    kept = [outs.pop(0) for _ in range(2 if receives else 0)]
    sent = [outs.pop(0) for _ in range(2 if sends else 0)]
    own = outs.pop(0) if sends else None
    sems = outs.pop(0)
    at = (place[0] * steps + step) * 2 * count
    slots = [(side, b) for side in range(2) for b in range(count)]
    loads, stores = [], []
    for side, b in slots:
        square = tab[at + side * count + b]
        if sends:
            loads.append(
                pltpu.make_async_copy(partial.at[square], own.at[side, b], sems.at[0, side, b])
            )
            loads[-1].start()
        if receives:
            stores.append(
                pltpu.make_async_copy(came[side].at[b], kept[side].at[square], sems.at[1, side, b])
            )
            stores[-1].start()
    if sends:
        for load, (side, b) in zip(loads, slots):
            load.wait()
            total = own[side, b]
            if receives:
                total = total + came[side][b].astype(F32)
            sent[side][b] = total.astype(BF16)
    for store in stores:
        store.wait()


def hop(table, place, steps, step, count, partial, received, kept, sends, after):
    size = partial.shape[1]
    inside = pl.BlockSpec(memory_space=pltpu.VMEM)
    anywhere = pl.BlockSpec(memory_space=pl.ANY)
    numbers = pl.BlockSpec(memory_space=pltpu.SMEM)
    receives = received is not None
    message = jax.ShapeDtypeStruct((count, size, size), BF16)
    in_specs, operands = [numbers, numbers], [table, place]
    out_specs, out_shape, aliases = [], [], {}
    if sends:
        in_specs += [anywhere]
        operands += [partial]
    if receives:
        aliases = {len(operands) + 2: 0, len(operands) + 3: 1}
        in_specs += [inside, inside, anywhere, anywhere]
        operands += [*received, *kept]
        out_specs += [anywhere, anywhere]
        out_shape += [jax.ShapeDtypeStruct(k.shape, k.dtype) for k in kept]
    in_specs += [anywhere] * len(after)
    operands += after
    scratch = []
    if sends:
        out_specs += [inside, inside]
        out_shape += [message, message]
        scratch = [pltpu.VMEM((2, count, size, size), F32)]
    found = pl.pallas_call(
        functools.partial(
            hop_kernel, receives, sends, (2 if receives else 0) + len(after), count, steps, step
        ),
        in_specs=in_specs,
        out_specs=out_specs,
        out_shape=out_shape,
        scratch_shapes=scratch + [pltpu.SemaphoreType.DMA((2, 2, count))],
        input_output_aliases=aliases,
        compiler_params=params(46 * 1024 * 1024),
        cost_estimate=pl.CostEstimate(
            flops=4 * count * size * size, bytes_accessed=20 * count * size * size, transcendentals=0
        ),
        name="hop",
    )(*operands)
    if receives:
        kept, found = found[:2], found[2:]
    return kept, (found if sends else None)


def column_half(slices, early, z):
    high = lax.div(2 * z, jnp.int32(slices))
    return 1 - high if early else high


def rows_kernel(slices, parts, span, part, local, early, tab, mode, place, *refs):
    n = slices // 2 * parts * 2
    own, right, left = refs[:n], refs[n : 2 * n], refs[2 * n : 3 * n]
    tiles = refs[-1].shape[4]
    out_ref = refs[-1].reshape(span * part * 2 * tiles, LANES)
    z, h = place[0], pl.program_id(0)
    first = column_half(slices, early, z) * (slices // 2)
    has_right, has_left = z > 0, z < slices - 1
    size = span * part

    def total(at):
        r = jnp.where(has_right, right[at][0].astype(F32), 0.0)
        l = jnp.where(has_left, left[at][0].astype(F32), 0.0)
        return own[at][0] + r + l

    for j in range(slices // 2):
        for k in range(parts):
            at = 2 * (j * parts + k)
            kind = mode[((z * parts + h) * slices + first + j) * parts + k]

            def put(ri, value, j=j, k=k):
                for d in range(span):
                    for e in range(span):
                        tile = (d * part * 2 + ri) * tiles + ((j * span + e) * local + k * part) // LANES
                        out_ref[pl.ds(tile, part, stride=2 * tiles), :] = value[
                            d * part : (d + 1) * part, e * part : (e + 1) * part
                        ]

            @pl.when(kind == 0)
            def _():
                put(0, total(at))
                put(1, total(at + 1))

            @pl.when(kind == 1)
            def _():
                put(0, total(at).T)
                put(1, -(total(at + 1).T))

            @pl.when(kind == 2)
            def _():
                direct = total(at)
                mirror = direct.T
                row = lax.broadcasted_iota(jnp.int32, (size, size), 0)
                col = lax.broadcasted_iota(jnp.int32, (size, size), 1)
                put(0, jnp.where(row >= col, direct, mirror))
                put(1, jnp.where(row < col, direct, jnp.where(row == col, 0.0, -mirror)))


def visibility_rows(plan, place, partial, kept, span, part, antennas, out):
    slices, parts = plan.slices, plan.parts
    size = span * part
    local = parts * part
    ids, modes = plan.outputs()
    early = out is None
    per_j = parts * 2
    per_half = slices // 2 * per_j

    def spec(at):
        return pl.BlockSpec(
            (1, size, size),
            lambda h, tab, mode, place: (
                tab[
                    (2 * (place[0] * parts + h) + column_half(slices, early, place[0])) * per_half + at
                ],
                0,
                0,
            ),
        )

    tiles = antennas // 2 // LANES
    again = [] if out is None else [out]
    operands = [partial] * per_half + [kept[0]] * per_half + [kept[1]] * per_half + again
    return pl.pallas_call(
        functools.partial(rows_kernel, slices, parts, span, part, local, early),
        grid_spec=pltpu.PrefetchScalarGridSpec(
            num_scalar_prefetch=3,
            grid=(parts,),
            in_specs=[spec(at) for _ in range(3) for at in range(per_half)]
            + [pl.BlockSpec(memory_space=pl.ANY) for _ in again],
            out_specs=pl.BlockSpec(
                (span, 1, part * 2, 1, tiles, LANES),
                lambda h, tab, mode, place: (0, h, 0, column_half(slices, early, place[0]), 0, 0),
            ),
        ),
        out_shape=jax.ShapeDtypeStruct((span, parts, part * 2, 2, tiles, LANES), F32),
        input_output_aliases={} if out is None else {3 + 3 * per_half: 0},
        compiler_params=params(),
        cost_estimate=pl.CostEstimate(
            flops=span * local * antennas * 4,
            bytes_accessed=span * local * antennas * 12,
            transcendentals=0,
        ),
        name="visibility_rows",
    )(jnp.asarray(ids.reshape(-1)), jnp.asarray(modes.reshape(-1)), place, *operands)


def on_device(voltages, filter_taps, antenna_flags):
    taps, length = filter_taps.shape
    channels, slices = lax.axis_size("chan"), lax.axis_size("tm")
    local = voltages.shape[1]
    samples = voltages.shape[2]
    frames = samples // length
    part = 128
    parts = local // part
    span = channels // slices

    head = taps * length
    halos = []
    for h in range(parts):
        tail = voltages[:, h * part : (h + 1) * part, samples - head :]
        halos.append(lax.ppermute(tail, "tm", [(i, i + 1) for i in range(slices - 1)]))
    weights = filterbank_weights(filter_taps, channels)
    scale = (antenna_flags.astype(F32) / math.sqrt(length)).reshape(1, local)

    plan = Plan(slices, parts, 4)
    table = jnp.asarray(plan.table())
    place = lax.axis_index("tm").astype(jnp.int32).reshape(1)
    weight = 1.0 / (frames * slices)
    antennas = channels * local
    spectra, token = [], weights
    for h in range(parts):
        pieces = 2 if h == 0 else 1
        chunk = frames // pieces
        found = []
        for t in reversed(range(pieces)):
            own, token = filterbank(
                voltages, halos[h], weights, scale, length, channels, part, h, t * chunk, chunk, token
            )
            found.insert(
                0, lax.all_to_all(own, "chan", split_axis=0, concat_axis=0, tiled=True)
            )
        spectra.append(found)

    work = [
        (call, h, k, low, min(low + 2, slices) if call == len(plan.calls) - 1 > 0 else slices)
        for call, (h, k) in enumerate(plan.calls)
        for low in (range(0, slices, 2) if call == len(plan.calls) - 1 > 0 else (0,))
    ]

    def extend(partial, kept, count):
        for _ in range(count):
            call, h, k, low, high = work.pop(0)
            made = correlate(
                partial, plan.total, slices, call, spectra[h], spectra[k], span, weight, h == k,
                low, high,
            )
            partial = made[0]
            if kept is None:
                kept = made[1:]
        return partial, kept

    def needed(step):
        must = sum(1 for item in work if item[0] <= plan.last_call(step))
        soon = any(item[0] <= plan.last_call(step + n) for item in work for n in (1, 2))
        return max(must, 1 if soon and step > 2 else 0)

    partial, kept = extend(None, None, 1)
    arrived, out = {}, None
    early = max(plan.first_ready(), plan.steps - 1)
    holds = []
    for step in range(plan.steps + 2):
        partial, kept = extend(partial, kept, needed(step))
        sends = step < plan.steps
        received = arrived.pop(step - 2, None)
        kept, outgoing = hop(
            table, place, plan.steps + 2, step, plan.count, partial, received, kept, sends, holds
        )
        holds = []
        if sends:
            right = [(p, p + 1) for p in plan.senders(plan.right, step)]
            end = slices - 1
            left = [(end - p, end - p - 1) for p in plan.senders(plan.left, step)]
            arrived[step] = [
                lax.ppermute(outgoing[0], "tm", right),
                lax.ppermute(outgoing[1], "tm", left),
            ]
        if step == early:
            out = visibility_rows(plan, place, partial, kept, span, part, antennas, None)
            holds = [out]
    out = visibility_rows(plan, place, partial, kept, span, part, antennas, out)
    return out.reshape(span * local, 2, 1, antennas)


def solution(mesh):
    placed = (P(None, "chan", "tm"), P(), P("chan"))
    return jax.shard_map(
        on_device,
        mesh=mesh,
        in_specs=placed,
        out_specs=P("tm", None, "chan", None),
        check_vma=False,
    )
```

```python
import functools
import math

import jax
import jax.numpy as jnp
import numpy as np
from jax import lax
from jax.experimental import pallas as pl
from jax.experimental.pallas import tpu as pltpu
from jax.sharding import PartitionSpec as P

F32, BF16 = jnp.float32, jnp.bfloat16
GROUP = 8
LANES = 128
FRAMES_PER_STEP = 128
VMEM_LIMIT = 52 * 1024 * 1024


def params(limit=VMEM_LIMIT):
    return pltpu.CompilerParams(vmem_limit_bytes=limit)


def weights_kernel(taps_ref, trig_ref, out_ref, wide):
    taps, length = taps_ref.shape
    rows = trig_ref.shape[0]
    size = GROUP * length
    flat = jnp.concatenate([taps_ref[taps - 1 - k : taps - k, :] for k in range(taps)], axis=1)
    base = flat * jnp.concatenate([trig_ref[...]] * taps, axis=1)
    for f in range(GROUP):
        before = jnp.zeros((rows, (f + 1) * length), F32)
        moved = [before, base]
        if f < GROUP - 1:
            moved.append(jnp.zeros((rows, (GROUP - 1 - f) * length), F32))
        moved = jnp.concatenate(moved, axis=1)
        for t in range(wide.shape[0]):
            wide[t, pl.ds(f, rows, stride=GROUP), :] = moved[:, t * LANES : (t + 1) * LANES]
    n = rows * GROUP
    each = size // LANES
    for t in range(wide.shape[0]):
        full = wide[t]
        high = full.astype(BF16)
        low = (full - high.astype(F32)).astype(BF16)
        m, lanes = t // each, slice(t % each * LANES, (t % each + 1) * LANES)
        out_ref[2 * m * n : (2 * m + 1) * n, lanes] = high
        out_ref[(2 * m + 1) * n : (2 * m + 2) * n, lanes] = low


def filterbank_weights(filter_taps, channels):
    taps, length = filter_taps.shape
    phase = np.arange(length)[None, :] * np.arange(channels)[:, None] % length
    angle = phase * (2.0 * math.pi / length)
    trig = np.stack([np.cos(angle), np.sin(angle)]).reshape(2 * channels, length)
    rows = 2 * channels * GROUP
    blocks = taps // GROUP + 1
    return pl.pallas_call(
        weights_kernel,
        out_shape=jax.ShapeDtypeStruct((blocks * 2 * rows, GROUP * length), BF16),
        scratch_shapes=[pltpu.VMEM((blocks * GROUP * length // LANES, rows, LANES), F32)],
        compiler_params=params(),
        name="weights",
    )(filter_taps, jnp.asarray(trig.astype(np.float32)))


def filterbank_kernel(channels, length, head_ref, v_ref, w_ref, s_ref, after_ref, out_ref, token_ref, carry, found):
    del after_ref, token_ref
    step = pl.program_id(0)
    _, part, lanes = v_ref.shape
    size = GROUP * length
    half = channels * GROUP
    rows = 2 * half
    blocks = w_ref.shape[0] // (2 * rows)
    scale = s_ref[...].astype(F32) / math.sqrt(length)

    def advance(ref, at):
        x = ref[:, :, at * size : (at + 1) * size].reshape(2 * part, size)
        r = lax.dot_general(w_ref[...], x, (((1,), (1,)), ((), ())), preferred_element_type=F32)
        third = [
            r[2 * m * rows : (2 * m + 1) * rows] + r[(2 * m + 1) * rows : (2 * m + 2) * rows]
            for m in range(blocks)
        ]
        done = carry[blocks - 2] + third[blocks - 1]
        for m in range(blocks - 2, 0, -1):
            carry[m] = carry[m - 1] + third[m]
        carry[0] = third[0]
        return done

    @pl.when(step == 0)
    def _():
        carry[...] = jnp.zeros_like(carry)
        for b in range(head_ref.shape[2] // size):
            advance(head_ref, b)

    for b in range(lanes // size):
        done = advance(v_ref, b)
        cos, sin = done[:half], done[half:]
        both = (
            (cos[:, :part] + sin[:, part:]) * scale,
            (cos[:, part:] - sin[:, :part]) * scale,
        )
        for c in range(channels):
            for ri in range(2):
                found[c, ri, b * GROUP : (b + 1) * GROUP, :] = both[ri][c * GROUP : (c + 1) * GROUP]
    for c in range(channels):
        for ri in range(2):
            out_ref[c, ri] = found[c, ri].T.astype(BF16)


def filterbank(voltages, halo, weights, scale, length, channels, part, h, start, frames, after):
    block = min(frames, FRAMES_PER_STEP)
    lanes = block * length
    head = halo.shape[2]
    first = start * length
    if start == 0:
        before, head_map = halo, lambda s: (0, 0, 0)
    else:
        before, head_map = voltages, lambda s: (0, h, first // head - 1)
    blocks = head // (GROUP * length)
    return pl.pallas_call(
        functools.partial(filterbank_kernel, channels, length),
        grid=(frames // block,),
        in_specs=[
            pl.BlockSpec((2, part, head), head_map),
            pl.BlockSpec((2, part, lanes), lambda s: (0, h, first // lanes + s)),
            pl.BlockSpec(weights.shape, lambda s: (0, 0)),
            pl.BlockSpec((1, part), lambda s: (0, h)),
            pl.BlockSpec(memory_space=pl.ANY),
        ],
        out_specs=[
            pl.BlockSpec((channels, 2, part, block), lambda s: (0, 0, 0, s)),
            pl.BlockSpec(memory_space=pl.ANY),
        ],
        out_shape=[
            jax.ShapeDtypeStruct((channels, 2, part, frames), BF16),
            jax.ShapeDtypeStruct((8, LANES), F32),
        ],
        scratch_shapes=[
            pltpu.VMEM((blocks, 2 * channels * GROUP, 2 * part), F32),
            pltpu.VMEM((channels, 2, block, part), F32),
        ],
        compiler_params=params(),
        cost_estimate=pl.CostEstimate(
            flops=2 * weights.size * 2 * part * frames // GROUP,
            bytes_accessed=2 * 2 * part * frames * length,
            transcendentals=0,
        ),
        name=f"filterbank_h{h}_f{start}",
    )(before, voltages, weights, scale, after)


def correlate_kernel(times, weight, fresh, same, low, first, *refs):
    xs, ys = refs[:times[0]], refs[times[0] : sum(times)]
    out_ref = refs[sum(times)] if fresh else refs[sum(times) + 1]
    i = pl.program_id(0) + low
    span, _, part, _ = xs[0].shape
    size = span * part
    group = ys[0].shape[0] // span

    def side(some, ri):
        wide = [jnp.concatenate([ref[d, ri] for d in range(ref.shape[0])], axis=0) for ref in some]
        return wide[0] if len(wide) == 1 else jnp.concatenate(wide, axis=1)

    real, imag = side(xs, 0), side(xs, 1)
    turned = jnp.concatenate(
        [jnp.concatenate([real, imag], axis=0), jnp.concatenate([imag, -real], axis=0)], axis=1
    )
    both = lax.dot_general(
        turned,
        jnp.concatenate([side(ys, 0), side(ys, 1)], axis=1),
        (((1,), (1,)), ((), ())),
        preferred_element_type=F32,
    )
    both = both * weight
    for n in range(group):
        columns = slice(n * size, (n + 1) * size)
        out_ref[2 * n] = both[:size, columns]
        out_ref[2 * n + 1] = both[size:, columns]
        if same:

            @pl.when(i == first + n)
            def _():
                row = lax.broadcasted_iota(jnp.int32, (size, size), 0)
                col = lax.broadcasted_iota(jnp.int32, (size, size), 1)
                out_ref[2 * n] = jnp.where(row >= col, both[:size, columns], both[size:, columns])


def correlate(partial, total, slices, call, xs, ys, span, weight, same, which):
    part = xs[0].shape[2]
    size = span * part
    frames = sum(x.shape[3] for x in xs)
    group = slices // 2
    low = which * group if same else 0
    rows = [
        pl.BlockSpec((span, 2, part, x.shape[3]), lambda i: (low + i, 0, 0, 0)) for x in xs
    ]
    columns = [
        pl.BlockSpec((group * span, 2, part, y.shape[3]), lambda i: (which, 0, 0, 0)) for y in ys
    ]
    out_block = pl.BlockSpec(
        (2 * group, size, size), lambda i: (2 * (call * slices + low + i) + which, 0, 0)
    )
    shape = jax.ShapeDtypeStruct((total, size, size), F32)
    store = jax.ShapeDtypeStruct((total, size, size), BF16)
    fresh = partial is None
    anywhere = pl.BlockSpec(memory_space=pl.ANY)
    return pl.pallas_call(
        functools.partial(
            correlate_kernel, (len(xs), len(ys)), weight, fresh, same, low, which * group
        ),
        grid=(slices - low,),
        in_specs=rows + columns + ([] if fresh else [anywhere]),
        out_specs=[out_block, anywhere, anywhere] if fresh else [out_block],
        out_shape=[shape, store, store] if fresh else [shape],
        input_output_aliases={} if fresh else {len(xs) + len(ys): 0},
        compiler_params=params(),
        cost_estimate=pl.CostEstimate(
            flops=8 * (slices - low) * group * size * size * frames,
            bytes_accessed=8 * (slices - low) * group * size * size,
            transcendentals=0,
        ),
        name="correlate",
    )(*xs, *ys, *([] if fresh else [partial]))


class Plan:
    def __init__(self, slices, parts, count):
        self.slices, self.parts, self.count = slices, parts, count
        self.calls = []
        self.pair_at = {}
        for h in range(parts):
            for k in range(h, -1, -1):
                first = len(self.calls) * slices * slices
                self.calls.append((h, k))
                for i in range(slices):
                    for j in range(slices):
                        if k < h or j <= i:
                            self.pair_at[h, i, k, j] = first + i * slices + j
        self.spare = 2 * len(self.calls) * slices * slices
        self.total = self.spare + 2 * count
        self.right = self.messages(lambda i, j: max(i, j))
        self.left = self.messages(lambda i, j: slices - 1 - min(i, j))
        self.steps = 0
        for index in range(2 * (len(self.right) + len(self.left)) + 4 * slices):
            if self.senders(self.right, index) or self.senders(self.left, index):
                self.steps = index + 1

    def squares(self, h, i, k, j):
        at = 2 * self.pair_at[h, i, k, j]
        return (at, at) if (h, i) == (k, j) else (at, at + 1)

    def messages(self, reach):
        queues, last = [[] for _ in self.calls], []
        for (h, i, k, j) in self.pair_at:
            far = reach(i, j)
            if far:
                late = self.late(i, j) and self.late(j, i)
                for square in sorted(set(self.squares(h, i, k, j))):
                    entry = (-far, late, self.work_of(h, k, j), square)
                    (queues[self.calls.index((h, k))] if far > 1 else last).append(entry)
        if self.slices == 2:
            queues, last = [last], []
        found = []
        for queue in [sorted(q) for q in queues] + [sorted(last)]:
            for at in range(0, len(queue), self.count):
                some = queue[at : at + self.count]
                ids = [entry[-1] for entry in some]
                found.append((ids, max(-entry[0] for entry in some)))
        return found

    def late(self, z, j):
        return (2 * z < self.slices) == (2 * j < self.slices)

    def first_ready(self):
        ready = 0
        ids, _ = self.outputs()
        for z in range(self.slices):
            for messages, place in ((self.right, z), (self.left, self.slices - 1 - z)):
                if place == 0:
                    continue
                for k, (squares, _) in enumerate(messages):
                    for j in range(self.slices):
                        if not self.late(z, j) and set(ids[z, :, j].ravel()) & set(squares):
                            ready = max(ready, k + 2 * place)
        return ready

    def senders(self, messages, step):
        places = []
        for place in range(self.slices - 1):
            k = step - 2 * place
            if 0 <= k < len(messages) and messages[k][1] > place:
                places.append(place)
        return places

    def table(self):
        rows = np.tile(
            self.spare + np.arange(2 * self.count, dtype=np.int32), (self.slices, self.steps + 2, 1)
        )
        for z in range(self.slices):
            for step in range(self.steps + 2):
                for side, (messages, place) in enumerate(
                    ((self.right, z), (self.left, self.slices - 1 - z))
                ):
                    k = step - 2 * place
                    if 0 <= k < len(messages):
                        for b, square in enumerate(messages[k][0]):
                            rows[z, step, side * self.count + b] = square
        return rows.reshape(-1)

    def work_of(self, h, k, j):
        return 2 * self.calls.index((h, k)) + 2 * j // self.slices

    def last_work(self, step):
        need = 0
        for messages in (self.right, self.left):
            for place in range(self.slices):
                k = step - 2 * place
                if 0 <= k < len(messages):
                    for square in messages[k][0]:
                        for (h, _, c, j), at in self.pair_at.items():
                            if at == square // 2:
                                need = max(need, self.work_of(h, c, j))
        return need

    def outputs(self):
        z_n, h_n = self.slices, self.parts
        ids = np.zeros((z_n, h_n, z_n, h_n, 2), np.int32)
        modes = np.zeros((z_n, h_n, z_n, h_n), np.int32)
        for z in range(z_n):
            for h in range(h_n):
                for j in range(z_n):
                    for k in range(h_n):
                        if (h, z, k, j) in self.pair_at:
                            ids[z, h, j, k] = self.squares(h, z, k, j)
                            modes[z, h, j, k] = 2 if (h, z) == (k, j) else 0
                        else:
                            ids[z, h, j, k] = self.squares(k, j, h, z)
                            modes[z, h, j, k] = 1
        return ids, modes


def hop_kernel(receives, sends, held, count, steps, step, tab, place, *refs):
    refs = list(refs)
    partial = refs.pop(0) if sends else None
    came = [refs.pop(0) for _ in range(2 if receives else 0)]
    outs = refs[held:]
    kept = [outs.pop(0) for _ in range(2 if receives else 0)]
    sent = [outs.pop(0) for _ in range(2 if sends else 0)]
    own = outs.pop(0) if sends else None
    sems = outs.pop(0)
    at = (place[0] * steps + step) * 2 * count
    slots = [(side, b) for side in range(2) for b in range(count)]
    loads, stores = [], []
    for side, b in slots:
        square = tab[at + side * count + b]
        if sends:
            loads.append(
                pltpu.make_async_copy(partial.at[square], own.at[side, b], sems.at[0, side, b])
            )
            loads[-1].start()
        if receives:
            stores.append(
                pltpu.make_async_copy(came[side].at[b], kept[side].at[square], sems.at[1, side, b])
            )
            stores[-1].start()
    if sends:
        for load, (side, b) in zip(loads, slots):
            load.wait()
            total = own[side, b]
            if receives:
                total = total + came[side][b].astype(F32)
            sent[side][b] = total.astype(BF16)
    for store in stores:
        store.wait()


def hop(table, place, steps, step, count, partial, received, kept, sends, after):
    size = partial.shape[1]
    inside = pl.BlockSpec(memory_space=pltpu.VMEM)
    anywhere = pl.BlockSpec(memory_space=pl.ANY)
    numbers = pl.BlockSpec(memory_space=pltpu.SMEM)
    receives = received is not None
    message = jax.ShapeDtypeStruct((count, size, size), BF16)
    in_specs, operands = [numbers, numbers], [table, place]
    out_specs, out_shape, aliases = [], [], {}
    if sends:
        in_specs += [anywhere]
        operands += [partial]
    if receives:
        aliases = {len(operands) + 2: 0, len(operands) + 3: 1}
        in_specs += [inside, inside, anywhere, anywhere]
        operands += [*received, *kept]
        out_specs += [anywhere, anywhere]
        out_shape += [jax.ShapeDtypeStruct(k.shape, k.dtype) for k in kept]
    in_specs += [anywhere] * len(after)
    operands += after
    scratch = []
    if sends:
        out_specs += [inside, inside]
        out_shape += [message, message]
        scratch = [pltpu.VMEM((2, count, size, size), F32)]
    found = pl.pallas_call(
        functools.partial(
            hop_kernel, receives, sends, (2 if receives else 0) + len(after), count, steps, step
        ),
        in_specs=in_specs,
        out_specs=out_specs,
        out_shape=out_shape,
        scratch_shapes=scratch + [pltpu.SemaphoreType.DMA((2, 2, count))],
        input_output_aliases=aliases,
        compiler_params=params(46 * 1024 * 1024),
        cost_estimate=pl.CostEstimate(
            flops=4 * count * size * size, bytes_accessed=20 * count * size * size, transcendentals=0
        ),
        name="hop",
    )(*operands)
    if receives:
        kept, found = found[:2], found[2:]
    return kept, (found if sends else None)


def column_half(slices, early, z):
    high = lax.div(2 * z, jnp.int32(slices))
    return 1 - high if early else high


def rows_kernel(slices, parts, span, part, local, early, tab, mode, place, *refs):
    n = slices // 2 * parts * 2
    own, right, left = refs[:n], refs[n : 2 * n], refs[2 * n : 3 * n]
    tiles = refs[-1].shape[4]
    out_ref = refs[-1].reshape(span * part * 2 * tiles, LANES)
    z, h = place[0], pl.program_id(0)
    first = column_half(slices, early, z) * (slices // 2)
    has_right, has_left = z > 0, z < slices - 1
    size = span * part

    def total(at):
        r = jnp.where(has_right, right[at][0].astype(F32), 0.0)
        l = jnp.where(has_left, left[at][0].astype(F32), 0.0)
        return own[at][0] + r + l

    for j in range(slices // 2):
        for k in range(parts):
            at = 2 * (j * parts + k)
            kind = mode[((z * parts + h) * slices + first + j) * parts + k]

            def put(ri, value, j=j, k=k):
                for d in range(span):
                    for e in range(span):
                        tile = (d * part * 2 + ri) * tiles + ((j * span + e) * local + k * part) // LANES
                        out_ref[pl.ds(tile, part, stride=2 * tiles), :] = value[
                            d * part : (d + 1) * part, e * part : (e + 1) * part
                        ]

            @pl.when(kind == 0)
            def _():
                put(0, total(at))
                put(1, total(at + 1))

            @pl.when(kind == 1)
            def _():
                put(0, total(at).T)
                put(1, -(total(at + 1).T))

            @pl.when(kind == 2)
            def _():
                direct = total(at)
                mirror = direct.T
                row = lax.broadcasted_iota(jnp.int32, (size, size), 0)
                col = lax.broadcasted_iota(jnp.int32, (size, size), 1)
                put(0, jnp.where(row >= col, direct, mirror))
                put(1, jnp.where(row < col, direct, jnp.where(row == col, 0.0, -mirror)))


def visibility_rows(plan, place, partial, kept, span, part, antennas, out):
    slices, parts = plan.slices, plan.parts
    size = span * part
    local = parts * part
    ids, modes = plan.outputs()
    early = out is None
    per_j = parts * 2
    per_half = slices // 2 * per_j

    def spec(at):
        return pl.BlockSpec(
            (1, size, size),
            lambda h, tab, mode, place: (
                tab[
                    (2 * (place[0] * parts + h) + column_half(slices, early, place[0])) * per_half + at
                ],
                0,
                0,
            ),
        )

    tiles = antennas // 2 // LANES
    again = [] if out is None else [out]
    operands = [partial] * per_half + [kept[0]] * per_half + [kept[1]] * per_half + again
    return pl.pallas_call(
        functools.partial(rows_kernel, slices, parts, span, part, local, early),
        grid_spec=pltpu.PrefetchScalarGridSpec(
            num_scalar_prefetch=3,
            grid=(parts,),
            in_specs=[spec(at) for _ in range(3) for at in range(per_half)]
            + [pl.BlockSpec(memory_space=pl.ANY) for _ in again],
            out_specs=pl.BlockSpec(
                (span, 1, part * 2, 1, tiles, LANES),
                lambda h, tab, mode, place: (0, h, 0, column_half(slices, early, place[0]), 0, 0),
            ),
        ),
        out_shape=jax.ShapeDtypeStruct((span, parts, part * 2, 2, tiles, LANES), F32),
        input_output_aliases={} if out is None else {3 + 3 * per_half: 0},
        compiler_params=params(),
        cost_estimate=pl.CostEstimate(
            flops=span * local * antennas * 4,
            bytes_accessed=span * local * antennas * 12,
            transcendentals=0,
        ),
        name="visibility_rows",
    )(jnp.asarray(ids.reshape(-1)), jnp.asarray(modes.reshape(-1)), place, *operands)


def on_device(voltages, filter_taps, antenna_flags):
    taps, length = filter_taps.shape
    channels, slices = lax.axis_size("chan"), lax.axis_size("tm")
    local = voltages.shape[1]
    samples = voltages.shape[2]
    frames = samples // length
    part = 128
    parts = local // part
    span = channels // slices

    head = taps * length
    halos = []
    for h in range(parts):
        tail = voltages[:, h * part : (h + 1) * part, samples - head :]
        halos.append(lax.ppermute(tail, "tm", [(i, i + 1) for i in range(slices - 1)]))
    weights = filterbank_weights(filter_taps, channels)
    scale = antenna_flags.reshape(1, local)

    plan = Plan(slices, parts, 4)
    table = jnp.asarray(plan.table())
    place = lax.axis_index("tm").astype(jnp.int32).reshape(1)
    weight = 1.0 / (frames * slices)
    antennas = channels * local
    spectra, token = [], weights
    for h in range(parts):
        pieces = 2 if h == 0 else 1
        chunk = frames // pieces
        found = []
        for t in reversed(range(pieces)):
            own, token = filterbank(
                voltages, halos[h], weights, scale, length, channels, part, h, t * chunk, chunk, token
            )
            found.insert(
                0, lax.all_to_all(own, "chan", split_axis=0, concat_axis=0, tiled=True)
            )
        spectra.append(found)

    done = []

    def extend(partial, kept, count):
        for _ in range(count):
            call, which = len(done) // 2, len(done) % 2
            h, k = plan.calls[call]
            made = correlate(
                partial, plan.total, slices, call, spectra[h], spectra[k], span, weight, h == k, which
            )
            partial = made[0]
            if kept is None:
                kept = made[1:]
            done.append(call)
        return partial, kept

    def needed(step):
        must = max(0, plan.last_work(step) + 1 - len(done))
        soon = len(done) <= plan.last_work(step + 1)
        early = soon and (len(done) < 2 or step > 3)
        return max(must, 1 if early else 0)

    partial, kept = None, None
    arrived, out = {}, None
    early = max(plan.first_ready(), plan.steps - 1)
    holds = []
    for step in range(plan.steps + 2):
        partial, kept = extend(partial, kept, needed(step))
        sends = step < plan.steps
        received = arrived.pop(step - 2, None)
        kept, outgoing = hop(
            table, place, plan.steps + 2, step, plan.count, partial, received, kept, sends, holds
        )
        holds = []
        if sends:
            right = [(p, p + 1) for p in plan.senders(plan.right, step)]
            end = slices - 1
            left = [(end - p, end - p - 1) for p in plan.senders(plan.left, step)]
            arrived[step] = [
                lax.ppermute(outgoing[0], "tm", right),
                lax.ppermute(outgoing[1], "tm", left),
            ]
        if step == early:
            out = visibility_rows(plan, place, partial, kept, span, part, antennas, None)
            holds = [out]
    out = visibility_rows(plan, place, partial, kept, span, part, antennas, out)
    return out.reshape(span * local, 2, 1, antennas)


def solution(mesh):
    placed = (P(None, "chan", "tm"), P(), P("chan"))
    return jax.shard_map(
        on_device,
        mesh=mesh,
        in_specs=placed,
        out_specs=P("tm", None, "chan", None),
        check_vma=False,
    )
```

```python
import functools
import math

import jax
import jax.numpy as jnp
import numpy as np
from jax import lax
from jax.experimental import pallas as pl
from jax.experimental.pallas import tpu as pltpu
from jax.sharding import PartitionSpec as P

F32, BF16 = jnp.float32, jnp.bfloat16
GROUP = 8
LANES = 128
FRAMES_PER_STEP = 128
VMEM_LIMIT = 52 * 1024 * 1024


def params(limit=VMEM_LIMIT):
    return pltpu.CompilerParams(vmem_limit_bytes=limit)


def weights_kernel(taps_ref, trig_ref, out_ref, wide):
    taps, length = taps_ref.shape
    rows = trig_ref.shape[0]
    size = GROUP * length
    flat = jnp.concatenate([taps_ref[taps - 1 - k : taps - k, :] for k in range(taps)], axis=1)
    base = flat * jnp.concatenate([trig_ref[...]] * taps, axis=1)
    for f in range(GROUP):
        before = jnp.zeros((rows, (f + 1) * length), F32)
        moved = [before, base]
        if f < GROUP - 1:
            moved.append(jnp.zeros((rows, (GROUP - 1 - f) * length), F32))
        moved = jnp.concatenate(moved, axis=1)
        for t in range(wide.shape[0]):
            wide[t, pl.ds(f, rows, stride=GROUP), :] = moved[:, t * LANES : (t + 1) * LANES]
    n = rows * GROUP
    each = size // LANES
    for t in range(wide.shape[0]):
        full = wide[t]
        high = full.astype(BF16).astype(F32)
        m, lanes = t // each, slice(t % each * LANES, (t % each + 1) * LANES)
        both = jnp.concatenate([high, full - high], axis=0).astype(BF16)
        out_ref[2 * m * n : 2 * (m + 1) * n, lanes] = both


def filterbank_weights(filter_taps, channels):
    taps, length = filter_taps.shape
    phase = np.arange(length)[None, :] * np.arange(channels)[:, None] % length
    angle = phase * (2.0 * math.pi / length)
    trig = np.stack([np.cos(angle), np.sin(angle)]).reshape(2 * channels, length)
    trig = np.delete(trig, channels, axis=0)
    rows = trig.shape[0] * GROUP
    blocks = taps // GROUP + 1
    return pl.pallas_call(
        weights_kernel,
        out_shape=jax.ShapeDtypeStruct((blocks * 2 * rows, GROUP * length), BF16),
        scratch_shapes=[pltpu.VMEM((blocks * GROUP * length // LANES, rows, LANES), F32)],
        compiler_params=params(),
        name="weights",
    )(filter_taps, jnp.asarray(trig.astype(np.float32)))


def filterbank_kernel(channels, length, head_ref, v_ref, w_ref, s_ref, after_ref, out_ref, token_ref, carry, found):
    del after_ref, token_ref
    step = pl.program_id(0)
    _, part, lanes = v_ref.shape
    size = GROUP * length
    half = channels * GROUP
    rows = carry.shape[1]
    blocks = w_ref.shape[0] // (2 * rows)
    scale = s_ref[...].astype(F32) / math.sqrt(length)

    def advance(ref, at):
        x = ref[:, :, at * size : (at + 1) * size].reshape(2 * part, size)
        r = lax.dot_general(w_ref[...], x, (((1,), (1,)), ((), ())), preferred_element_type=F32)
        third = [
            r[2 * m * rows : (2 * m + 1) * rows] + r[(2 * m + 1) * rows : (2 * m + 2) * rows]
            for m in range(blocks)
        ]
        done = carry[blocks - 2] + third[blocks - 1]
        for m in range(blocks - 2, 0, -1):
            carry[m] = carry[m - 1] + third[m]
        carry[0] = third[0]
        return done

    @pl.when(step == 0)
    def _():
        carry[...] = jnp.zeros_like(carry)
        for b in range(head_ref.shape[2] // size):
            advance(head_ref, b)

    for b in range(lanes // size):
        done = advance(v_ref, b)
        cos, sin = done[:half], done[half:]
        for c in range(channels):
            at = slice(c * GROUP, (c + 1) * GROUP)
            real, imag = cos[at, :part], cos[at, part:]
            if c > 0:
                at = slice((c - 1) * GROUP, c * GROUP)
                real, imag = real + sin[at, part:], imag - sin[at, :part]
            found[c, 0, b * GROUP : (b + 1) * GROUP, :] = real * scale
            found[c, 1, b * GROUP : (b + 1) * GROUP, :] = imag * scale
    for c in range(channels):
        for ri in range(2):
            out_ref[c, ri] = found[c, ri].T.astype(BF16)


def filterbank(voltages, halo, weights, scale, length, channels, part, h, start, frames, after):
    block = min(frames, FRAMES_PER_STEP)
    lanes = block * length
    head = halo.shape[2]
    first = start * length
    if start == 0:
        before, head_map = halo, lambda s: (0, 0, 0)
    else:
        before, head_map = voltages, lambda s: (0, h, first // head - 1)
    blocks = head // (GROUP * length)
    return pl.pallas_call(
        functools.partial(filterbank_kernel, channels, length),
        grid=(frames // block,),
        in_specs=[
            pl.BlockSpec((2, part, head), head_map),
            pl.BlockSpec((2, part, lanes), lambda s: (0, h, first // lanes + s)),
            pl.BlockSpec(weights.shape, lambda s: (0, 0)),
            pl.BlockSpec((1, part), lambda s: (0, h)),
            pl.BlockSpec(memory_space=pl.ANY),
        ],
        out_specs=[
            pl.BlockSpec((channels, 2, part, block), lambda s: (0, 0, 0, s)),
            pl.BlockSpec(memory_space=pl.ANY),
        ],
        out_shape=[
            jax.ShapeDtypeStruct((channels, 2, part, frames), BF16),
            jax.ShapeDtypeStruct((8, LANES), F32),
        ],
        scratch_shapes=[
            pltpu.VMEM((blocks, (2 * channels - 1) * GROUP, 2 * part), F32),
            pltpu.VMEM((channels, 2, block, part), F32),
        ],
        compiler_params=params(),
        cost_estimate=pl.CostEstimate(
            flops=2 * weights.size * 2 * part * frames // GROUP,
            bytes_accessed=2 * 2 * part * frames * length,
            transcendentals=0,
        ),
        name=f"filterbank_h{h}_f{start}",
    )(before, voltages, weights, scale, after)


def correlate_kernel(times, span, weight, fresh, same, low, first, *refs):
    xs, ys = refs[:times[0]], refs[times[0] : sum(times)]
    out_ref = refs[sum(times)] if fresh else refs[sum(times) + 1]
    part = xs[0].shape[2]
    size = span * part
    group = ys[0].shape[0] // span
    many = xs[0].shape[0] // span

    def side(some, start, count, ri):
        wide = [
            jnp.concatenate([ref[start + d, ri] for d in range(count)], axis=0) for ref in some
        ]
        return wide[0] if len(wide) == 1 else jnp.concatenate(wide, axis=1)

    on_real, on_imag = [], []
    for n in range(many):
        real, imag = side(xs, n * span, span, 0), side(xs, n * span, span, 1)
        on_real += [real, imag]
        on_imag += [imag, -real]
    turned = jnp.concatenate(
        [jnp.concatenate(on_real, axis=0), jnp.concatenate(on_imag, axis=0)], axis=1
    )
    other = [side(ys, 0, group * span, ri) for ri in range(2)]
    both = lax.dot_general(
        turned,
        jnp.concatenate(other, axis=1),
        (((1,), (1,)), ((), ())),
        preferred_element_type=F32,
    )
    both = both * weight
    for m in range(many):
        i = pl.program_id(0) * many + low + m
        real = both[2 * m * size : (2 * m + 1) * size]
        imag = both[(2 * m + 1) * size : (2 * m + 2) * size]
        for n in range(group):
            columns = slice(n * size, (n + 1) * size)
            out_ref[m, 2 * n] = real[:, columns]
            out_ref[m, 2 * n + 1] = imag[:, columns]
            if same:

                @pl.when(i == first + n)
                def _():
                    row = lax.broadcasted_iota(jnp.int32, (size, size), 0)
                    col = lax.broadcasted_iota(jnp.int32, (size, size), 1)
                    out_ref[m, 2 * n] = jnp.where(row >= col, real[:, columns], imag[:, columns])


def correlate(partial, total, slices, call, xs, ys, span, weight, same, which):
    part = xs[0].shape[2]
    size = span * part
    frames = sum(x.shape[3] for x in xs)
    group = slices // 2
    low = which * group if same else 0
    many = 2 if low % 2 == 0 else 1
    rows = [
        pl.BlockSpec((many * span, 2, part, x.shape[3]), lambda i: (low // many + i, 0, 0, 0))
        for x in xs
    ]
    columns = [
        pl.BlockSpec((group * span, 2, part, y.shape[3]), lambda i: (which, 0, 0, 0)) for y in ys
    ]
    out_block = pl.BlockSpec(
        (many, 2 * group, size, size), lambda i: ((call * slices + low) // many + i, which, 0, 0)
    )
    lines = total // (2 * slices)
    shape = jax.ShapeDtypeStruct((lines, 2 * slices, size, size), F32)
    store = jax.ShapeDtypeStruct((total, size, size), BF16)
    fresh = partial is None
    if not fresh:
        partial = partial.reshape(shape.shape)
    anywhere = pl.BlockSpec(memory_space=pl.ANY)
    made = pl.pallas_call(
        functools.partial(
            correlate_kernel, (len(xs), len(ys)), span, weight, fresh, same, low, which * group
        ),
        grid=((slices - low) // many,),
        in_specs=rows + columns + ([] if fresh else [anywhere]),
        out_specs=[out_block, anywhere, anywhere] if fresh else [out_block],
        out_shape=[shape, store, store] if fresh else [shape],
        input_output_aliases={} if fresh else {len(xs) + len(ys): 0},
        compiler_params=params(),
        cost_estimate=pl.CostEstimate(
            flops=8 * (slices - low) * group * size * size * frames,
            bytes_accessed=8 * (slices - low) * group * size * size,
            transcendentals=0,
        ),
        name="correlate",
    )(*xs, *ys, *([] if fresh else [partial]))
    return [made[0].reshape(total, size, size)] + list(made[1:])


class Plan:
    def __init__(self, slices, parts, count):
        self.slices, self.parts, self.count = slices, parts, count
        self.calls = []
        self.pair_at = {}
        for h in range(parts):
            for k in range(h, -1, -1):
                first = len(self.calls) * slices * slices
                self.calls.append((h, k))
                for i in range(slices):
                    for j in range(slices):
                        if k < h or j <= i:
                            self.pair_at[h, i, k, j] = first + i * slices + j
        self.spare = 2 * len(self.calls) * slices * slices
        self.total = self.spare + -(-2 * count // (2 * slices)) * 2 * slices
        self.right = self.messages(lambda i, j: max(i, j))
        self.left = self.messages(lambda i, j: slices - 1 - min(i, j))
        self.steps = 0
        for index in range(2 * (len(self.right) + len(self.left)) + 4 * slices):
            if self.senders(self.right, index) or self.senders(self.left, index):
                self.steps = index + 1

    def squares(self, h, i, k, j):
        at = 2 * self.pair_at[h, i, k, j]
        return (at, at) if (h, i) == (k, j) else (at, at + 1)

    def messages(self, reach):
        queues, last = [[] for _ in self.calls], []
        for (h, i, k, j) in self.pair_at:
            far = reach(i, j)
            if far:
                late = self.late(i, j) and self.late(j, i)
                for square in sorted(set(self.squares(h, i, k, j))):
                    if far == 1:
                        late = self.only_last(h, i, k, j)
                    entry = (-far, late, self.work_of(h, k, j), square)
                    (queues[self.calls.index((h, k))] if far > 1 else last).append(entry)
        if self.slices == 2:
            queues, last = [last], []
        found = []
        for queue in [sorted(q) for q in queues] + [sorted(last)]:
            for at in range(0, len(queue), self.count):
                some = queue[at : at + self.count]
                ids = [entry[-1] for entry in some]
                found.append((ids, max(-entry[0] for entry in some)))
        return found

    def late(self, z, j):
        return (2 * z < self.slices) == (2 * j < self.slices)

    def only_last(self, h, i, k, j):
        near = (1, self.slices - 2)
        touched = [part for part, z in ((h, i), (k, j)) if z in near]
        return all(part == self.parts - 1 for part in touched)

    def first_ready(self):
        ready = 0
        ids, _ = self.outputs()
        for z in range(self.slices):
            for messages, place in ((self.right, z), (self.left, self.slices - 1 - z)):
                if place == 0:
                    continue
                for k, (squares, _) in enumerate(messages):
                    for j in range(self.slices):
                        parts = self.parts - 1 if self.late(z, j) else self.parts
                        if set(ids[z, :parts, j].ravel()) & set(squares):
                            ready = max(ready, k + 2 * place)
        return ready

    def senders(self, messages, step):
        places = []
        for place in range(self.slices - 1):
            k = step - 2 * place
            if 0 <= k < len(messages) and messages[k][1] > place:
                places.append(place)
        return places

    def table(self):
        rows = np.tile(
            self.spare + np.arange(2 * self.count, dtype=np.int32), (self.slices, self.steps + 2, 1)
        )
        for z in range(self.slices):
            for step in range(self.steps + 2):
                for side, (messages, place) in enumerate(
                    ((self.right, z), (self.left, self.slices - 1 - z))
                ):
                    k = step - 2 * place
                    if 0 <= k < len(messages):
                        for b, square in enumerate(messages[k][0]):
                            rows[z, step, side * self.count + b] = square
        return rows.reshape(-1)

    def work_of(self, h, k, j):
        return 2 * self.calls.index((h, k)) + 2 * j // self.slices

    def last_work(self, step):
        need = 0
        for messages in (self.right, self.left):
            for place in range(self.slices):
                k = step - 2 * place
                if 0 <= k < len(messages):
                    for square in messages[k][0]:
                        for (h, _, c, j), at in self.pair_at.items():
                            if at == square // 2:
                                need = max(need, self.work_of(h, c, j))
        return need

    def outputs(self):
        z_n, h_n = self.slices, self.parts
        ids = np.zeros((z_n, h_n, z_n, h_n, 2), np.int32)
        modes = np.zeros((z_n, h_n, z_n, h_n), np.int32)
        for z in range(z_n):
            for h in range(h_n):
                for j in range(z_n):
                    for k in range(h_n):
                        if (h, z, k, j) in self.pair_at:
                            ids[z, h, j, k] = self.squares(h, z, k, j)
                            modes[z, h, j, k] = 2 if (h, z) == (k, j) else 0
                        else:
                            ids[z, h, j, k] = self.squares(k, j, h, z)
                            modes[z, h, j, k] = 1
        return ids, modes


def hop_kernel(receives, sends, held, count, steps, step, tab, place, *refs):
    refs = list(refs)
    partial = refs.pop(0) if sends else None
    came = [refs.pop(0) for _ in range(2 if receives else 0)]
    outs = refs[held:]
    kept = [outs.pop(0) for _ in range(2 if receives else 0)]
    sent = [outs.pop(0) for _ in range(2 if sends else 0)]
    own = outs.pop(0) if sends else None
    sems = outs.pop(0)
    at = (place[0] * steps + step) * 2 * count
    slots = [(side, b) for side in range(2) for b in range(count)]
    loads, stores = [], []
    for side, b in slots:
        square = tab[at + side * count + b]
        if sends:
            loads.append(
                pltpu.make_async_copy(partial.at[square], own.at[side, b], sems.at[0, side, b])
            )
            loads[-1].start()
        if receives:
            stores.append(
                pltpu.make_async_copy(came[side].at[b], kept[side].at[square], sems.at[1, side, b])
            )
            stores[-1].start()
    if sends:
        for load, (side, b) in zip(loads, slots):
            load.wait()
            total = own[side, b]
            if receives:
                total = total + came[side][b].astype(F32)
            sent[side][b] = total.astype(BF16)
    for store in stores:
        store.wait()


def hop(table, place, steps, step, count, partial, received, kept, sends, after):
    size = partial.shape[1]
    inside = pl.BlockSpec(memory_space=pltpu.VMEM)
    anywhere = pl.BlockSpec(memory_space=pl.ANY)
    numbers = pl.BlockSpec(memory_space=pltpu.SMEM)
    receives = received is not None
    message = jax.ShapeDtypeStruct((count, size, size), BF16)
    in_specs, operands = [numbers, numbers], [table, place]
    out_specs, out_shape, aliases = [], [], {}
    if sends:
        in_specs += [anywhere]
        operands += [partial]
    if receives:
        aliases = {len(operands) + 2: 0, len(operands) + 3: 1}
        in_specs += [inside, inside, anywhere, anywhere]
        operands += [*received, *kept]
        out_specs += [anywhere, anywhere]
        out_shape += [jax.ShapeDtypeStruct(k.shape, k.dtype) for k in kept]
    in_specs += [anywhere] * len(after)
    operands += after
    scratch = []
    if sends:
        out_specs += [inside, inside]
        out_shape += [message, message]
        scratch = [pltpu.VMEM((2, count, size, size), F32)]
    found = pl.pallas_call(
        functools.partial(
            hop_kernel, receives, sends, (2 if receives else 0) + len(after), count, steps, step
        ),
        in_specs=in_specs,
        out_specs=out_specs,
        out_shape=out_shape,
        scratch_shapes=scratch + [pltpu.SemaphoreType.DMA((2, 2, count))],
        input_output_aliases=aliases,
        compiler_params=params(46 * 1024 * 1024),
        cost_estimate=pl.CostEstimate(
            flops=4 * count * size * size, bytes_accessed=20 * count * size * size, transcendentals=0
        ),
        name="hop",
    )(*operands)
    if receives:
        kept, found = found[:2], found[2:]
    return kept, (found if sends else None)


def piece(slices, parts, early, z, step):
    high = lax.div(2 * z, jnp.int32(slices))
    if not early:
        return parts - 1, high
    return lax.rem(step, jnp.int32(parts)), jnp.where(step < parts, 1 - high, high)


def rows_kernel(slices, parts, span, part, local, early, tab, mode, place, *refs):
    n = slices // 2 * parts * 2
    own, right, left = refs[:n], refs[n : 2 * n], refs[2 * n : 3 * n]
    tiles = refs[-1].shape[4]
    out_ref = refs[-1].reshape(span * part * 2 * tiles, LANES)
    z = place[0]
    h, half = piece(slices, parts, early, z, pl.program_id(0))
    first = half * (slices // 2)
    has_right, has_left = z > 0, z < slices - 1
    size = span * part

    def total(at):
        r = jnp.where(has_right, right[at][0].astype(F32), 0.0)
        l = jnp.where(has_left, left[at][0].astype(F32), 0.0)
        return own[at][0] + r + l

    for j in range(slices // 2):
        for k in range(parts):
            at = 2 * (j * parts + k)
            kind = mode[((z * parts + h) * slices + first + j) * parts + k]

            def put(ri, value, j=j, k=k):
                for d in range(span):
                    for e in range(span):
                        tile = (d * part * 2 + ri) * tiles + ((j * span + e) * local + k * part) // LANES
                        out_ref[pl.ds(tile, part, stride=2 * tiles), :] = value[
                            d * part : (d + 1) * part, e * part : (e + 1) * part
                        ]

            @pl.when(kind == 0)
            def _():
                put(0, total(at))
                put(1, total(at + 1))

            @pl.when(kind == 1)
            def _():
                put(0, total(at).T)
                put(1, -(total(at + 1).T))

            @pl.when(kind == 2)
            def _():
                direct = total(at)
                mirror = direct.T
                row = lax.broadcasted_iota(jnp.int32, (size, size), 0)
                col = lax.broadcasted_iota(jnp.int32, (size, size), 1)
                put(0, jnp.where(row >= col, direct, mirror))
                put(1, jnp.where(row < col, direct, jnp.where(row == col, 0.0, -mirror)))


def visibility_rows(plan, place, partial, kept, span, part, antennas, out):
    slices, parts = plan.slices, plan.parts
    size = span * part
    local = parts * part
    ids, modes = plan.outputs()
    early = out is None
    per_j = parts * 2
    per_half = slices // 2 * per_j

    def start(s, place):
        h, half = piece(slices, parts, early, place[0], s)
        return 2 * (place[0] * parts + h) + half

    def out_map(s, tab, mode, place):
        h, half = piece(slices, parts, early, place[0], s)
        return 0, h, 0, half, 0, 0

    def spec(at):
        return pl.BlockSpec(
            (1, size, size),
            lambda s, tab, mode, place: (tab[start(s, place) * per_half + at], 0, 0),
        )

    tiles = antennas // 2 // LANES
    again = [] if out is None else [out]
    operands = [partial] * per_half + [kept[0]] * per_half + [kept[1]] * per_half + again
    return pl.pallas_call(
        functools.partial(rows_kernel, slices, parts, span, part, local, early),
        grid_spec=pltpu.PrefetchScalarGridSpec(
            num_scalar_prefetch=3,
            grid=(2 * parts - 1 if early else 1,),
            in_specs=[spec(at) for _ in range(3) for at in range(per_half)]
            + [pl.BlockSpec(memory_space=pl.ANY) for _ in again],
            out_specs=pl.BlockSpec(
                (span, 1, part * 2, 1, tiles, LANES), out_map
            ),
        ),
        out_shape=jax.ShapeDtypeStruct((span, parts, part * 2, 2, tiles, LANES), F32),
        input_output_aliases={} if out is None else {3 + 3 * per_half: 0},
        compiler_params=params(),
        cost_estimate=pl.CostEstimate(
            flops=span * local * antennas * 4,
            bytes_accessed=span * local * antennas * 12,
            transcendentals=0,
        ),
        name="visibility_rows",
    )(jnp.asarray(ids.reshape(-1)), jnp.asarray(modes.reshape(-1)), place, *operands)


def on_device(voltages, filter_taps, antenna_flags):
    taps, length = filter_taps.shape
    channels, slices = lax.axis_size("chan"), lax.axis_size("tm")
    local = voltages.shape[1]
    samples = voltages.shape[2]
    frames = samples // length
    part = 128
    parts = local // part
    span = channels // slices

    head = taps * length
    halos = []
    for h in range(parts):
        tail = voltages[:, h * part : (h + 1) * part, samples - head :]
        halos.append(lax.ppermute(tail, "tm", [(i, i + 1) for i in range(slices - 1)]))
    weights = filterbank_weights(filter_taps, channels)
    scale = antenna_flags.reshape(1, local)

    plan = Plan(slices, parts, 4)
    table = jnp.asarray(plan.table())
    place = lax.axis_index("tm").astype(jnp.int32).reshape(1)
    weight = 1.0 / (frames * slices)
    antennas = channels * local
    spectra, token = [], weights
    for h in range(parts):
        pieces = 2 if h == 0 else 1
        chunk = frames // pieces
        found = []
        for t in reversed(range(pieces)):
            own, token = filterbank(
                voltages, halos[h], weights, scale, length, channels, part, h, t * chunk, chunk, token
            )
            found.insert(
                0, lax.all_to_all(own, "chan", split_axis=0, concat_axis=0, tiled=True)
            )
        spectra.append(found)

    done = []

    def extend(partial, kept, count):
        for _ in range(count):
            call, which = len(done) // 2, len(done) % 2
            h, k = plan.calls[call]
            made = correlate(
                partial, plan.total, slices, call, spectra[h], spectra[k], span, weight, h == k, which
            )
            partial = made[0]
            if kept is None:
                kept = made[1:]
            done.append(call)
        return partial, kept

    def needed(step):
        must = max(0, plan.last_work(step) + 1 - len(done))
        soon = len(done) <= plan.last_work(step + 1)
        early = soon and (len(done) < 2 or step > 3)
        return max(must, 1 if early else 0)

    partial, kept = None, None
    arrived, out = {}, None
    early = max(plan.first_ready(), plan.steps - 1)
    holds = []
    for step in range(plan.steps + 2):
        partial, kept = extend(partial, kept, needed(step))
        sends = step < plan.steps
        received = arrived.pop(step - 2, None)
        kept, outgoing = hop(
            table, place, plan.steps + 2, step, plan.count, partial, received, kept, sends, holds
        )
        holds = []
        if sends:
            right = [(p, p + 1) for p in plan.senders(plan.right, step)]
            end = slices - 1
            left = [(end - p, end - p - 1) for p in plan.senders(plan.left, step)]
            arrived[step] = [
                lax.ppermute(outgoing[0], "tm", right),
                lax.ppermute(outgoing[1], "tm", left),
            ]
        if step == early:
            out = visibility_rows(plan, place, partial, kept, span, part, antennas, None)
            holds = [out]
    out = visibility_rows(plan, place, partial, kept, span, part, antennas, out)
    return out.reshape(span * local, 2, 1, antennas)


def solution(mesh):
    placed = (P(None, "chan", "tm"), P(), P("chan"))
    return jax.shard_map(
        on_device,
        mesh=mesh,
        in_specs=placed,
        out_specs=P("tm", None, "chan", None),
        check_vma=False,
    )
```

```python
import functools
import math

import jax
import jax.numpy as jnp
import numpy as np
from jax import lax
from jax.experimental import pallas as pl
from jax.experimental.pallas import tpu as pltpu
from jax.sharding import PartitionSpec as P

F32, BF16 = jnp.float32, jnp.bfloat16
GROUP = 8
LANES = 128
FRAMES_PER_STEP = 128
VMEM_LIMIT = 52 * 1024 * 1024


def params(limit=VMEM_LIMIT):
    return pltpu.CompilerParams(vmem_limit_bytes=limit)


def weights_kernel(taps_ref, trig_ref, out_ref, wide):
    taps, length = taps_ref.shape
    rows = trig_ref.shape[0]
    size = GROUP * length
    flat = jnp.concatenate([taps_ref[taps - 1 - k : taps - k, :] for k in range(taps)], axis=1)
    base = flat * jnp.concatenate([trig_ref[...]] * taps, axis=1)
    for f in range(GROUP):
        before = jnp.zeros((rows, (f + 1) * length), F32)
        moved = [before, base]
        if f < GROUP - 1:
            moved.append(jnp.zeros((rows, (GROUP - 1 - f) * length), F32))
        moved = jnp.concatenate(moved, axis=1)
        for t in range(wide.shape[0]):
            wide[t, pl.ds(f, rows, stride=GROUP), :] = moved[:, t * LANES : (t + 1) * LANES]
    n = rows * GROUP
    each = size // LANES
    for t in range(wide.shape[0]):
        full = wide[t]
        high = full.astype(BF16).astype(F32)
        m, lanes = t // each, slice(t % each * LANES, (t % each + 1) * LANES)
        both = jnp.concatenate([high, full - high], axis=0).astype(BF16)
        out_ref[2 * m * n : 2 * (m + 1) * n, lanes] = both


def filterbank_weights(filter_taps, channels):
    taps, length = filter_taps.shape
    phase = np.arange(length)[None, :] * np.arange(channels)[:, None] % length
    angle = phase * (2.0 * math.pi / length)
    trig = np.stack([np.cos(angle), np.sin(angle)]).reshape(2 * channels, length)
    trig = np.delete(trig, channels, axis=0)
    rows = trig.shape[0] * GROUP
    blocks = taps // GROUP + 1
    return pl.pallas_call(
        weights_kernel,
        out_shape=jax.ShapeDtypeStruct((blocks * 2 * rows, GROUP * length), BF16),
        scratch_shapes=[pltpu.VMEM((blocks * GROUP * length // LANES, rows, LANES), F32)],
        compiler_params=params(),
        name="weights",
    )(filter_taps, jnp.asarray(trig.astype(np.float32)))


def filterbank_kernel(channels, length, head_ref, v_ref, w_ref, s_ref, after_ref, out_ref, token_ref, carry, found):
    del after_ref, token_ref
    step = pl.program_id(0)
    _, part, lanes = v_ref.shape
    size = GROUP * length
    half = channels * GROUP
    rows = carry.shape[1]
    blocks = w_ref.shape[0] // (2 * rows)
    scale = s_ref[...].astype(F32) / math.sqrt(length)

    def advance(ref, at):
        x = ref[:, :, at * size : (at + 1) * size].reshape(2 * part, size)
        r = lax.dot_general(w_ref[...], x, (((1,), (1,)), ((), ())), preferred_element_type=F32)
        third = [
            r[2 * m * rows : (2 * m + 1) * rows] + r[(2 * m + 1) * rows : (2 * m + 2) * rows]
            for m in range(blocks)
        ]
        done = carry[blocks - 2] + third[blocks - 1]
        for m in range(blocks - 2, 0, -1):
            carry[m] = carry[m - 1] + third[m]
        carry[0] = third[0]
        return done

    @pl.when(step == 0)
    def _():
        carry[...] = jnp.zeros_like(carry)
        for b in range(head_ref.shape[2] // size):
            advance(head_ref, b)

    for b in range(lanes // size):
        done = advance(v_ref, b)
        cos, sin = done[:half], done[half:]
        for c in range(channels):
            at = slice(c * GROUP, (c + 1) * GROUP)
            real, imag = cos[at, :part], cos[at, part:]
            if c > 0:
                at = slice((c - 1) * GROUP, c * GROUP)
                real, imag = real + sin[at, part:], imag - sin[at, :part]
            found[c, 0, b * GROUP : (b + 1) * GROUP, :] = real * scale
            found[c, 1, b * GROUP : (b + 1) * GROUP, :] = imag * scale
    for c in range(channels):
        for ri in range(2):
            out_ref[c, ri] = found[c, ri].T.astype(BF16)


def filterbank(voltages, halo, weights, scale, length, channels, part, h, start, frames, after):
    block = min(frames, FRAMES_PER_STEP)
    lanes = block * length
    head = halo.shape[2]
    first = start * length
    if start == 0:
        before, head_map = halo, lambda s: (0, 0, 0)
    else:
        before, head_map = voltages, lambda s: (0, h, first // head - 1)
    blocks = head // (GROUP * length)
    return pl.pallas_call(
        functools.partial(filterbank_kernel, channels, length),
        grid=(frames // block,),
        in_specs=[
            pl.BlockSpec((2, part, head), head_map),
            pl.BlockSpec((2, part, lanes), lambda s: (0, h, first // lanes + s)),
            pl.BlockSpec(weights.shape, lambda s: (0, 0)),
            pl.BlockSpec((1, part), lambda s: (0, h)),
            pl.BlockSpec(memory_space=pl.ANY),
        ],
        out_specs=[
            pl.BlockSpec((channels, 2, part, block), lambda s: (0, 0, 0, s)),
            pl.BlockSpec(memory_space=pl.ANY),
        ],
        out_shape=[
            jax.ShapeDtypeStruct((channels, 2, part, frames), BF16),
            jax.ShapeDtypeStruct((8, LANES), F32),
        ],
        scratch_shapes=[
            pltpu.VMEM((blocks, (2 * channels - 1) * GROUP, 2 * part), F32),
            pltpu.VMEM((channels, 2, block, part), F32),
        ],
        compiler_params=params(),
        cost_estimate=pl.CostEstimate(
            flops=2 * weights.size * 2 * part * frames // GROUP,
            bytes_accessed=2 * 2 * part * frames * length,
            transcendentals=0,
        ),
        name=f"filterbank_h{h}_f{start}",
    )(before, voltages, weights, scale, after)


def correlate_kernel(times, span, weight, fresh, same, low, first, *refs):
    xs, ys = refs[:times[0]], refs[times[0] : sum(times)]
    out_ref = refs[sum(times)] if fresh else refs[sum(times) + 1]
    part = xs[0].shape[2]
    size = span * part
    group = ys[0].shape[0] // span
    many = xs[0].shape[0] // span

    def side(some, start, count, ri):
        wide = [
            jnp.concatenate([ref[start + d, ri] for d in range(count)], axis=0) for ref in some
        ]
        return wide[0] if len(wide) == 1 else jnp.concatenate(wide, axis=1)

    on_real, on_imag = [], []
    for n in range(many):
        real, imag = side(xs, n * span, span, 0), side(xs, n * span, span, 1)
        on_real += [real, imag]
        on_imag += [imag, -real]
    turned = jnp.concatenate(
        [jnp.concatenate(on_real, axis=0), jnp.concatenate(on_imag, axis=0)], axis=1
    )
    other = [side(ys, 0, group * span, ri) for ri in range(2)]
    both = lax.dot_general(
        turned,
        jnp.concatenate(other, axis=1),
        (((1,), (1,)), ((), ())),
        preferred_element_type=F32,
    )
    both = both * weight
    for m in range(many):
        i = pl.program_id(0) * many + low + m
        real = both[2 * m * size : (2 * m + 1) * size]
        imag = both[(2 * m + 1) * size : (2 * m + 2) * size]
        for n in range(group):
            columns = slice(n * size, (n + 1) * size)
            out_ref[m, 2 * n] = real[:, columns]
            out_ref[m, 2 * n + 1] = imag[:, columns]
            if same:

                @pl.when(i == first + n)
                def _():
                    row = lax.broadcasted_iota(jnp.int32, (size, size), 0)
                    col = lax.broadcasted_iota(jnp.int32, (size, size), 1)
                    out_ref[m, 2 * n] = jnp.where(row >= col, real[:, columns], imag[:, columns])


def correlate(partial, total, slices, call, xs, ys, span, weight, same, which, upper):
    part = xs[0].shape[2]
    size = span * part
    frames = sum(x.shape[3] for x in xs)
    group = slices // 2
    low = upper * group
    many = 1
    rows = [
        pl.BlockSpec((many * span, 2, part, x.shape[3]), lambda i: (low // many + i, 0, 0, 0))
        for x in xs
    ]
    columns = [
        pl.BlockSpec((group * span, 2, part, y.shape[3]), lambda i: (which, 0, 0, 0)) for y in ys
    ]
    out_block = pl.BlockSpec(
        (many, 2 * group, size, size), lambda i: ((call * slices + low) // many + i, which, 0, 0)
    )
    lines = total // (2 * slices)
    shape = jax.ShapeDtypeStruct((lines, 2 * slices, size, size), F32)
    store = jax.ShapeDtypeStruct((total, size, size), BF16)
    fresh = partial is None
    if not fresh:
        partial = partial.reshape(shape.shape)
    anywhere = pl.BlockSpec(memory_space=pl.ANY)
    made = pl.pallas_call(
        functools.partial(
            correlate_kernel, (len(xs), len(ys)), span, weight, fresh, same, low, which * group
        ),
        grid=(group // many,),
        in_specs=rows + columns + ([] if fresh else [anywhere]),
        out_specs=[out_block, anywhere, anywhere] if fresh else [out_block],
        out_shape=[shape, store, store] if fresh else [shape],
        input_output_aliases={} if fresh else {len(xs) + len(ys): 0},
        compiler_params=params(),
        cost_estimate=pl.CostEstimate(
            flops=8 * group * group * size * size * frames,
            bytes_accessed=8 * group * group * size * size,
            transcendentals=0,
        ),
        name="correlate",
    )(*xs, *ys, *([] if fresh else [partial]))
    return [made[0].reshape(total, size, size)] + list(made[1:])


class Plan:
    def __init__(self, slices, parts, count):
        self.slices, self.parts, self.count = slices, parts, count
        self.calls = []
        self.pair_at = {}
        for h in range(parts):
            for k in range(h, -1, -1):
                first = len(self.calls) * slices * slices
                self.calls.append((h, k))
                for i in range(slices):
                    for j in range(slices):
                        if k < h or j <= i:
                            self.pair_at[h, i, k, j] = first + i * slices + j
        self.work = []
        for call, (h, k) in enumerate(self.calls):
            quarters = [(0, 1), (0, 0), (1, 1)] if h == k else [(0, 1), (1, 0), (1, 1), (0, 0)]
            self.work += [(call, which, upper) for which, upper in quarters]
        self.spare = 2 * len(self.calls) * slices * slices
        self.total = self.spare + -(-2 * count // (2 * slices)) * 2 * slices
        self.right = self.messages(lambda i, j: max(i, j))
        self.left = self.messages(lambda i, j: slices - 1 - min(i, j))
        self.steps = 0
        for index in range(2 * (len(self.right) + len(self.left)) + 4 * slices):
            if self.senders(self.right, index) or self.senders(self.left, index):
                self.steps = index + 1

    def squares(self, h, i, k, j):
        at = 2 * self.pair_at[h, i, k, j]
        return (at, at) if (h, i) == (k, j) else (at, at + 1)

    def messages(self, reach):
        queues, last = [[] for _ in self.calls], []
        for (h, i, k, j) in self.pair_at:
            far = reach(i, j)
            if far:
                late = self.late(i, j) and self.late(j, i)
                for square in sorted(set(self.squares(h, i, k, j))):
                    if far == 1:
                        late = self.only_last(h, i, k, j)
                    order = (-far, late, self.work_of(h, i, k, j))
                    if far > 1 and h == k:
                        order = (order[2],) + order[:2]
                    entry = order + (far, square)
                    (queues[self.calls.index((h, k))] if far > 1 else last).append(entry)
        if self.slices == 2:
            queues, last = [last], []
        found = []
        for queue in [sorted(q) for q in queues] + [sorted(last)]:
            for at in range(0, len(queue), self.count):
                some = queue[at : at + self.count]
                ids = [entry[-1] for entry in some]
                found.append((ids, max(entry[-2] for entry in some)))
        return found

    def late(self, z, j):
        return (2 * z < self.slices) == (2 * j < self.slices)

    def only_last(self, h, i, k, j):
        near = (1, self.slices - 2)
        touched = [part for part, z in ((h, i), (k, j)) if z in near]
        return all(part == self.parts - 1 for part in touched)

    def first_ready(self):
        ready = 0
        ids, _ = self.outputs()
        for z in range(self.slices):
            for messages, place in ((self.right, z), (self.left, self.slices - 1 - z)):
                if place == 0:
                    continue
                for k, (squares, _) in enumerate(messages):
                    for j in range(self.slices):
                        parts = self.parts - 1 if self.late(z, j) else self.parts
                        if set(ids[z, :parts, j].ravel()) & set(squares):
                            ready = max(ready, k + 2 * place)
        return ready

    def senders(self, messages, step):
        places = []
        for place in range(self.slices - 1):
            k = step - 2 * place
            if 0 <= k < len(messages) and messages[k][1] > place:
                places.append(place)
        return places

    def table(self):
        rows = np.tile(
            self.spare + np.arange(2 * self.count, dtype=np.int32), (self.slices, self.steps + 2, 1)
        )
        for z in range(self.slices):
            for step in range(self.steps + 2):
                for side, (messages, place) in enumerate(
                    ((self.right, z), (self.left, self.slices - 1 - z))
                ):
                    k = step - 2 * place
                    if 0 <= k < len(messages):
                        for b, square in enumerate(messages[k][0]):
                            rows[z, step, side * self.count + b] = square
        return rows.reshape(-1)

    def work_of(self, h, i, k, j):
        n = self.slices
        return self.work.index((self.calls.index((h, k)), 2 * j // n, 2 * i // n))

    def last_work(self, step):
        need = 0
        for messages in (self.right, self.left):
            for place in range(self.slices):
                k = step - 2 * place
                if 0 <= k < len(messages):
                    for square in messages[k][0]:
                        for (h, i, c, j), at in self.pair_at.items():
                            if at == square // 2:
                                need = max(need, self.work_of(h, i, c, j))
        return need

    def outputs(self):
        z_n, h_n = self.slices, self.parts
        ids = np.zeros((z_n, h_n, z_n, h_n, 2), np.int32)
        modes = np.zeros((z_n, h_n, z_n, h_n), np.int32)
        for z in range(z_n):
            for h in range(h_n):
                for j in range(z_n):
                    for k in range(h_n):
                        if (h, z, k, j) in self.pair_at:
                            ids[z, h, j, k] = self.squares(h, z, k, j)
                            modes[z, h, j, k] = 2 if (h, z) == (k, j) else 0
                        else:
                            ids[z, h, j, k] = self.squares(k, j, h, z)
                            modes[z, h, j, k] = 1
        return ids, modes


def hop_kernel(receives, sends, held, count, steps, step, tab, place, *refs):
    refs = list(refs)
    partial = refs.pop(0) if sends else None
    came = [refs.pop(0) for _ in range(2 if receives else 0)]
    outs = refs[held:]
    kept = [outs.pop(0) for _ in range(2 if receives else 0)]
    sent = [outs.pop(0) for _ in range(2 if sends else 0)]
    own = outs.pop(0) if sends else None
    sems = outs.pop(0)
    at = (place[0] * steps + step) * 2 * count
    slots = [(side, b) for side in range(2) for b in range(count)]
    loads, stores = [], []
    for side, b in slots:
        square = tab[at + side * count + b]
        if sends:
            loads.append(
                pltpu.make_async_copy(partial.at[square], own.at[side, b], sems.at[0, side, b])
            )
            loads[-1].start()
        if receives:
            stores.append(
                pltpu.make_async_copy(came[side].at[b], kept[side].at[square], sems.at[1, side, b])
            )
            stores[-1].start()
    if sends:
        for load, (side, b) in zip(loads, slots):
            load.wait()
            total = own[side, b]
            if receives:
                total = total + came[side][b].astype(F32)
            sent[side][b] = total.astype(BF16)
    for store in stores:
        store.wait()


def hop(table, place, steps, step, count, partial, received, kept, sends, after):
    size = partial.shape[1]
    inside = pl.BlockSpec(memory_space=pltpu.VMEM)
    anywhere = pl.BlockSpec(memory_space=pl.ANY)
    numbers = pl.BlockSpec(memory_space=pltpu.SMEM)
    receives = received is not None
    message = jax.ShapeDtypeStruct((count, size, size), BF16)
    in_specs, operands = [numbers, numbers], [table, place]
    out_specs, out_shape, aliases = [], [], {}
    if sends:
        in_specs += [anywhere]
        operands += [partial]
    if receives:
        aliases = {len(operands) + 2: 0, len(operands) + 3: 1}
        in_specs += [inside, inside, anywhere, anywhere]
        operands += [*received, *kept]
        out_specs += [anywhere, anywhere]
        out_shape += [jax.ShapeDtypeStruct(k.shape, k.dtype) for k in kept]
    in_specs += [anywhere] * len(after)
    operands += after
    scratch = []
    if sends:
        out_specs += [inside, inside]
        out_shape += [message, message]
        scratch = [pltpu.VMEM((2, count, size, size), F32)]
    found = pl.pallas_call(
        functools.partial(
            hop_kernel, receives, sends, (2 if receives else 0) + len(after), count, steps, step
        ),
        in_specs=in_specs,
        out_specs=out_specs,
        out_shape=out_shape,
        scratch_shapes=scratch + [pltpu.SemaphoreType.DMA((2, 2, count))],
        input_output_aliases=aliases,
        compiler_params=params(46 * 1024 * 1024),
        cost_estimate=pl.CostEstimate(
            flops=4 * count * size * size, bytes_accessed=20 * count * size * size, transcendentals=0
        ),
        name="hop",
    )(*operands)
    if receives:
        kept, found = found[:2], found[2:]
    return kept, (found if sends else None)


def piece(slices, parts, early, z, step):
    high = lax.div(2 * z, jnp.int32(slices))
    if not early:
        return parts - 1, high
    return lax.rem(step, jnp.int32(parts)), jnp.where(step < parts, 1 - high, high)


def rows_kernel(slices, parts, span, part, local, early, tab, mode, place, *refs):
    n = slices // 2 * parts * 2
    own, right, left = refs[:n], refs[n : 2 * n], refs[2 * n : 3 * n]
    tiles = refs[-1].shape[4]
    out_ref = refs[-1].reshape(span * part * 2 * tiles, LANES)
    z = place[0]
    h, half = piece(slices, parts, early, z, pl.program_id(0))
    first = half * (slices // 2)
    has_right, has_left = z > 0, z < slices - 1
    size = span * part

    def total(at):
        r = jnp.where(has_right, right[at][0].astype(F32), 0.0)
        l = jnp.where(has_left, left[at][0].astype(F32), 0.0)
        return own[at][0] + r + l

    for j in range(slices // 2):
        for k in range(parts):
            at = 2 * (j * parts + k)
            kind = mode[((z * parts + h) * slices + first + j) * parts + k]

            def put(ri, value, j=j, k=k):
                for d in range(span):
                    for e in range(span):
                        tile = (d * part * 2 + ri) * tiles + ((j * span + e) * local + k * part) // LANES
                        out_ref[pl.ds(tile, part, stride=2 * tiles), :] = value[
                            d * part : (d + 1) * part, e * part : (e + 1) * part
                        ]

            @pl.when(kind == 0)
            def _():
                put(0, total(at))
                put(1, total(at + 1))

            @pl.when(kind == 1)
            def _():
                put(0, total(at).T)
                put(1, -(total(at + 1).T))

            @pl.when(kind == 2)
            def _():
                direct = total(at)
                mirror = direct.T
                row = lax.broadcasted_iota(jnp.int32, (size, size), 0)
                col = lax.broadcasted_iota(jnp.int32, (size, size), 1)
                put(0, jnp.where(row >= col, direct, mirror))
                put(1, jnp.where(row < col, direct, jnp.where(row == col, 0.0, -mirror)))


def visibility_rows(plan, place, partial, kept, span, part, antennas, out):
    slices, parts = plan.slices, plan.parts
    size = span * part
    local = parts * part
    ids, modes = plan.outputs()
    early = out is None
    per_j = parts * 2
    per_half = slices // 2 * per_j

    def start(s, place):
        h, half = piece(slices, parts, early, place[0], s)
        return 2 * (place[0] * parts + h) + half

    def out_map(s, tab, mode, place):
        h, half = piece(slices, parts, early, place[0], s)
        return 0, h, 0, half, 0, 0

    def spec(at):
        return pl.BlockSpec(
            (1, size, size),
            lambda s, tab, mode, place: (tab[start(s, place) * per_half + at], 0, 0),
        )

    tiles = antennas // 2 // LANES
    again = [] if out is None else [out]
    operands = [partial] * per_half + [kept[0]] * per_half + [kept[1]] * per_half + again
    return pl.pallas_call(
        functools.partial(rows_kernel, slices, parts, span, part, local, early),
        grid_spec=pltpu.PrefetchScalarGridSpec(
            num_scalar_prefetch=3,
            grid=(2 * parts - 1 if early else 1,),
            in_specs=[spec(at) for _ in range(3) for at in range(per_half)]
            + [pl.BlockSpec(memory_space=pl.ANY) for _ in again],
            out_specs=pl.BlockSpec(
                (span, 1, part * 2, 1, tiles, LANES), out_map
            ),
        ),
        out_shape=jax.ShapeDtypeStruct((span, parts, part * 2, 2, tiles, LANES), F32),
        input_output_aliases={} if out is None else {3 + 3 * per_half: 0},
        compiler_params=params(),
        cost_estimate=pl.CostEstimate(
            flops=span * local * antennas * 4,
            bytes_accessed=span * local * antennas * 12,
            transcendentals=0,
        ),
        name="visibility_rows",
    )(jnp.asarray(ids.reshape(-1)), jnp.asarray(modes.reshape(-1)), place, *operands)


def on_device(voltages, filter_taps, antenna_flags):
    taps, length = filter_taps.shape
    channels, slices = lax.axis_size("chan"), lax.axis_size("tm")
    local = voltages.shape[1]
    samples = voltages.shape[2]
    frames = samples // length
    part = 128
    parts = local // part
    span = channels // slices

    head = taps * length
    halos = []
    for h in range(parts):
        tail = voltages[:, h * part : (h + 1) * part, samples - head :]
        halos.append(lax.ppermute(tail, "tm", [(i, i + 1) for i in range(slices - 1)]))
    weights = filterbank_weights(filter_taps, channels)
    scale = antenna_flags.reshape(1, local)

    plan = Plan(slices, parts, 4)
    table = jnp.asarray(plan.table())
    place = lax.axis_index("tm").astype(jnp.int32).reshape(1)
    weight = 1.0 / (frames * slices)
    antennas = channels * local
    spectra, token = [], weights
    for h in range(parts):
        pieces = 2 if h == 0 else 1
        chunk = frames // pieces
        found = []
        for t in reversed(range(pieces)):
            own, token = filterbank(
                voltages, halos[h], weights, scale, length, channels, part, h, t * chunk, chunk, token
            )
            found.insert(
                0, lax.all_to_all(own, "chan", split_axis=0, concat_axis=0, tiled=True)
            )
        spectra.append(found)

    done = []

    def extend(partial, kept, count):
        for _ in range(count):
            call, which, upper = plan.work[len(done)]
            h, k = plan.calls[call]
            made = correlate(
                partial, plan.total, slices, call, spectra[h], spectra[k], span, weight, h == k,
                which, upper,
            )
            partial = made[0]
            if kept is None:
                kept = made[1:]
            done.append(call)
        return partial, kept

    def needed(step):
        must = max(0, plan.last_work(step) + 1 - len(done))
        soon = len(done) < len(plan.work) and len(done) <= plan.last_work(step + 1)
        early = soon and step != 0 and (plan.work[len(done)][0] == 0 or step > 3)
        return max(must, 1 if early else 0)

    partial, kept = None, None
    arrived, out = {}, None
    early = max(plan.first_ready(), plan.steps - 1)
    holds = []
    for step in range(plan.steps + 2):
        partial, kept = extend(partial, kept, needed(step))
        sends = step < plan.steps
        received = arrived.pop(step - 2, None)
        kept, outgoing = hop(
            table, place, plan.steps + 2, step, plan.count, partial, received, kept, sends, holds
        )
        holds = []
        if sends:
            right = [(p, p + 1) for p in plan.senders(plan.right, step)]
            end = slices - 1
            left = [(end - p, end - p - 1) for p in plan.senders(plan.left, step)]
            arrived[step] = [
                lax.ppermute(outgoing[0], "tm", right),
                lax.ppermute(outgoing[1], "tm", left),
            ]
        if step == early:
            out = visibility_rows(plan, place, partial, kept, span, part, antennas, None)
            holds = [out]
    out = visibility_rows(plan, place, partial, kept, span, part, antennas, out)
    return out.reshape(span * local, 2, 1, antennas)


def solution(mesh):
    placed = (P(None, "chan", "tm"), P(), P("chan"))
    return jax.shard_map(
        on_device,
        mesh=mesh,
        in_specs=placed,
        out_specs=P("tm", None, "chan", None),
        check_vma=False,
    )
```

```python
import functools
import math

import jax
import jax.numpy as jnp
import numpy as np
from jax import lax
from jax.experimental import pallas as pl
from jax.experimental.pallas import tpu as pltpu
from jax.sharding import PartitionSpec as P

F32, BF16 = jnp.float32, jnp.bfloat16
GROUP = 8
LANES = 128
FRAMES_PER_STEP = 128
VMEM_LIMIT = 52 * 1024 * 1024


def params(limit=VMEM_LIMIT):
    return pltpu.CompilerParams(vmem_limit_bytes=limit)


def weights_kernel(taps_ref, trig_ref, out_ref, wide):
    taps, length = taps_ref.shape
    rows = trig_ref.shape[0]
    size = GROUP * length
    flat = jnp.concatenate([taps_ref[taps - 1 - k : taps - k, :] for k in range(taps)], axis=1)
    base = flat * jnp.concatenate([trig_ref[...]] * taps, axis=1)
    for f in range(GROUP):
        before = jnp.zeros((rows, (f + 1) * length), F32)
        moved = [before, base]
        if f < GROUP - 1:
            moved.append(jnp.zeros((rows, (GROUP - 1 - f) * length), F32))
        moved = jnp.concatenate(moved, axis=1)
        for t in range(wide.shape[0]):
            wide[t, pl.ds(f, rows, stride=GROUP), :] = moved[:, t * LANES : (t + 1) * LANES]
    n = rows * GROUP
    each = size // LANES
    for t in range(wide.shape[0]):
        full = wide[t]
        high = full.astype(BF16).astype(F32)
        m, lanes = t // each, slice(t % each * LANES, (t % each + 1) * LANES)
        both = jnp.concatenate([high, full - high], axis=0).astype(BF16)
        out_ref[2 * m * n : 2 * (m + 1) * n, lanes] = both


def filterbank_weights(filter_taps, channels):
    taps, length = filter_taps.shape
    phase = np.arange(length)[None, :] * np.arange(channels)[:, None] % length
    angle = phase * (2.0 * math.pi / length)
    trig = np.stack([np.cos(angle), np.sin(angle)]).reshape(2 * channels, length)
    trig = np.delete(trig, channels, axis=0)
    rows = trig.shape[0] * GROUP
    blocks = taps // GROUP + 1
    return pl.pallas_call(
        weights_kernel,
        out_shape=jax.ShapeDtypeStruct((blocks * 2 * rows, GROUP * length), BF16),
        scratch_shapes=[pltpu.VMEM((blocks * GROUP * length // LANES, rows, LANES), F32)],
        compiler_params=params(),
        name="weights",
    )(filter_taps, jnp.asarray(trig.astype(np.float32)))


def filterbank_kernel(channels, length, head_ref, v_ref, w_ref, s_ref, after_ref, out_ref, token_ref, carry, found):
    del after_ref, token_ref
    step = pl.program_id(0)
    _, part, lanes = v_ref.shape
    size = GROUP * length
    half = channels * GROUP
    rows = carry.shape[1]
    blocks = w_ref.shape[0] // (2 * rows)
    scale = s_ref[...].astype(F32) / math.sqrt(length)

    def advance(ref, at):
        x = ref[:, :, at * size : (at + 1) * size].reshape(2 * part, size)
        r = lax.dot_general(w_ref[...], x, (((1,), (1,)), ((), ())), preferred_element_type=F32)
        third = [
            r[2 * m * rows : (2 * m + 1) * rows] + r[(2 * m + 1) * rows : (2 * m + 2) * rows]
            for m in range(blocks)
        ]
        done = carry[blocks - 2] + third[blocks - 1]
        for m in range(blocks - 2, 0, -1):
            carry[m] = carry[m - 1] + third[m]
        carry[0] = third[0]
        return done

    @pl.when(step == 0)
    def _():
        carry[...] = jnp.zeros_like(carry)
        for b in range(head_ref.shape[2] // size):
            advance(head_ref, b)

    for b in range(lanes // size):
        done = advance(v_ref, b)
        cos, sin = done[:half], done[half:]
        for c in range(channels):
            at = slice(c * GROUP, (c + 1) * GROUP)
            real, imag = cos[at, :part], cos[at, part:]
            if c > 0:
                at = slice((c - 1) * GROUP, c * GROUP)
                real, imag = real + sin[at, part:], imag - sin[at, :part]
            found[c, 0, b * GROUP : (b + 1) * GROUP, :] = real * scale
            found[c, 1, b * GROUP : (b + 1) * GROUP, :] = imag * scale
    for c in range(channels):
        for ri in range(2):
            out_ref[c, ri] = found[c, ri].T.astype(BF16)


def filterbank(voltages, halo, weights, scale, length, channels, part, h, start, frames, after):
    block = min(frames, FRAMES_PER_STEP)
    lanes = block * length
    head = halo.shape[2]
    first = start * length
    if start == 0:
        before, head_map = halo, lambda s: (0, 0, 0)
    else:
        before, head_map = voltages, lambda s: (0, h, first // head - 1)
    blocks = head // (GROUP * length)
    return pl.pallas_call(
        functools.partial(filterbank_kernel, channels, length),
        grid=(frames // block,),
        in_specs=[
            pl.BlockSpec((2, part, head), head_map),
            pl.BlockSpec((2, part, lanes), lambda s: (0, h, first // lanes + s)),
            pl.BlockSpec(weights.shape, lambda s: (0, 0)),
            pl.BlockSpec((1, part), lambda s: (0, h)),
            pl.BlockSpec(memory_space=pl.ANY),
        ],
        out_specs=[
            pl.BlockSpec((channels, 2, part, block), lambda s: (0, 0, 0, s)),
            pl.BlockSpec(memory_space=pl.ANY),
        ],
        out_shape=[
            jax.ShapeDtypeStruct((channels, 2, part, frames), BF16),
            jax.ShapeDtypeStruct((8, LANES), F32),
        ],
        scratch_shapes=[
            pltpu.VMEM((blocks, (2 * channels - 1) * GROUP, 2 * part), F32),
            pltpu.VMEM((channels, 2, block, part), F32),
        ],
        compiler_params=params(),
        cost_estimate=pl.CostEstimate(
            flops=2 * weights.size * 2 * part * frames // GROUP,
            bytes_accessed=2 * 2 * part * frames * length,
            transcendentals=0,
        ),
        name=f"filterbank_h{h}_f{start}",
    )(before, voltages, weights, scale, after)


def correlate_kernel(times, span, weight, fresh, same, low, first, *refs):
    xs, ys = refs[:times[0]], refs[times[0] : sum(times)]
    out_ref = refs[sum(times)] if fresh else refs[sum(times) + 1]
    part = xs[0].shape[2]
    size = span * part
    group = ys[0].shape[0] // span
    many = xs[0].shape[0] // span

    def side(some, start, count, ri):
        wide = [
            jnp.concatenate([ref[start + d, ri] for d in range(count)], axis=0) for ref in some
        ]
        return wide[0] if len(wide) == 1 else jnp.concatenate(wide, axis=1)

    on_real, on_imag = [], []
    for n in range(many):
        real, imag = side(xs, n * span, span, 0), side(xs, n * span, span, 1)
        on_real += [real, imag]
        on_imag += [imag, -real]
    turned = jnp.concatenate(
        [jnp.concatenate(on_real, axis=0), jnp.concatenate(on_imag, axis=0)], axis=1
    )
    other = [side(ys, 0, group * span, ri) for ri in range(2)]
    both = lax.dot_general(
        turned,
        jnp.concatenate(other, axis=1),
        (((1,), (1,)), ((), ())),
        preferred_element_type=F32,
    )
    both = both * weight
    for m in range(many):
        i = pl.program_id(0) * many + low + m
        real = both[2 * m * size : (2 * m + 1) * size]
        imag = both[(2 * m + 1) * size : (2 * m + 2) * size]
        for n in range(group):
            columns = slice(n * size, (n + 1) * size)
            out_ref[m, 2 * n] = real[:, columns]
            out_ref[m, 2 * n + 1] = imag[:, columns]
            if same:

                @pl.when(i == first + n)
                def _():
                    row = lax.broadcasted_iota(jnp.int32, (size, size), 0)
                    col = lax.broadcasted_iota(jnp.int32, (size, size), 1)
                    out_ref[m, 2 * n] = jnp.where(row >= col, real[:, columns], imag[:, columns])


def correlate(partial, total, slices, call, xs, ys, span, weight, same, which, upper):
    part = xs[0].shape[2]
    size = span * part
    frames = sum(x.shape[3] for x in xs)
    group = slices // 2
    low = upper * group
    many = 1
    rows = [
        pl.BlockSpec((many * span, 2, part, x.shape[3]), lambda i: (low // many + i, 0, 0, 0))
        for x in xs
    ]
    columns = [
        pl.BlockSpec((group * span, 2, part, y.shape[3]), lambda i: (which, 0, 0, 0)) for y in ys
    ]
    out_block = pl.BlockSpec(
        (many, 2 * group, size, size), lambda i: ((call * slices + low) // many + i, which, 0, 0)
    )
    lines = total // (2 * slices)
    shape = jax.ShapeDtypeStruct((lines, 2 * slices, size, size), F32)
    store = jax.ShapeDtypeStruct((total, size, size), BF16)
    fresh = partial is None
    if not fresh:
        partial = partial.reshape(shape.shape)
    anywhere = pl.BlockSpec(memory_space=pl.ANY)
    made = pl.pallas_call(
        functools.partial(
            correlate_kernel, (len(xs), len(ys)), span, weight, fresh, same, low, which * group
        ),
        grid=(group // many,),
        in_specs=rows + columns + ([] if fresh else [anywhere]),
        out_specs=[out_block, anywhere, anywhere] if fresh else [out_block],
        out_shape=[shape, store, store] if fresh else [shape],
        input_output_aliases={} if fresh else {len(xs) + len(ys): 0},
        compiler_params=params(),
        cost_estimate=pl.CostEstimate(
            flops=8 * group * group * size * size * frames,
            bytes_accessed=8 * group * group * size * size,
            transcendentals=0,
        ),
        name="correlate",
    )(*xs, *ys, *([] if fresh else [partial]))
    return [made[0].reshape(total, size, size)] + list(made[1:])


class Plan:
    def __init__(self, slices, parts, count):
        self.slices, self.parts, self.count = slices, parts, count
        self.calls = []
        self.pair_at = {}
        for h in range(parts):
            for k in range(h, -1, -1):
                first = len(self.calls) * slices * slices
                self.calls.append((h, k))
                for i in range(slices):
                    for j in range(slices):
                        if k < h or j <= i:
                            self.pair_at[h, i, k, j] = first + i * slices + j
        self.work = []
        for call, (h, k) in enumerate(self.calls):
            quarters = [(0, 1), (0, 0), (1, 1)] if h == k else [(0, 1), (1, 0), (1, 1), (0, 0)]
            self.work += [(call, which, upper) for which, upper in quarters]
        self.spare = 2 * len(self.calls) * slices * slices
        self.total = self.spare + -(-2 * count // (2 * slices)) * 2 * slices
        self.right = self.messages(lambda i, j: max(i, j))
        self.left = self.messages(lambda i, j: slices - 1 - min(i, j))
        self.steps = 0
        for index in range(2 * (len(self.right) + len(self.left)) + 4 * slices):
            if self.senders(self.right, index) or self.senders(self.left, index):
                self.steps = index + 1

    def squares(self, h, i, k, j):
        at = 2 * self.pair_at[h, i, k, j]
        return (at, at) if (h, i) == (k, j) else (at, at + 1)

    def messages(self, reach):
        slices = self.slices
        queues, last = [[] for _ in self.calls], []
        for (h, i, k, j) in self.pair_at:
            far = reach(i, j)
            if far:
                late = self.late(i, j) and self.late(j, i)
                for square in sorted(set(self.squares(h, i, k, j))):
                    if far == 1:
                        late = self.only_last(h, i, k, j)
                    order = (-far, late, self.work_of(h, i, k, j))
                    if far > 1 and h == k:
                        order = (order[2],) + order[:2]
                    elif far > 1:
                        first = self.work_of(self.calls[-1][0], slices - 1, self.calls[-1][1], 0)
                        if far == slices - 1:
                            after = late and self.ends_last(h, i, k, j, reach)
                            order = (2 if late else 0, after, order[2])
                        elif order[2] == first and not late:
                            order = (1, False, order[2])
                        else:
                            order = (2 + slices - far, late, order[2])
                    entry = order + (far, square)
                    (queues[self.calls.index((h, k))] if far > 1 else last).append(entry)
        if self.slices == 2:
            queues, last = [last], []
        found = []
        for queue in [sorted(q) for q in queues] + [sorted(last)]:
            for at in range(0, len(queue), self.count):
                some = queue[at : at + self.count]
                ids = [entry[-1] for entry in some]
                found.append((ids, max(entry[-2] for entry in some)))
        return found

    def late(self, z, j):
        return (2 * z < self.slices) == (2 * j < self.slices)

    def only_last(self, h, i, k, j):
        near = (1, self.slices - 2)
        touched = [part for part, z in ((h, i), (k, j)) if z in near]
        return all(part == self.parts - 1 for part in touched)

    def ends_last(self, h, i, k, j, reach):
        end = self.slices - 1 if reach(self.slices - 1, 0) > reach(0, 0) else 0
        touched = [part for part, z in ((h, i), (k, j)) if z == end]
        return all(part == self.parts - 1 for part in touched)

    def first_ready(self):
        ready = 0
        ids, _ = self.outputs()
        for z in range(self.slices):
            for messages, place in ((self.right, z), (self.left, self.slices - 1 - z)):
                if place == 0:
                    continue
                for k, (squares, _) in enumerate(messages):
                    for j in range(self.slices):
                        parts = self.parts - 1 if self.late(z, j) else self.parts
                        if set(ids[z, :parts, j].ravel()) & set(squares):
                            ready = max(ready, k + 2 * place)
        return ready

    def senders(self, messages, step):
        places = []
        for place in range(self.slices - 1):
            k = step - 2 * place
            if 0 <= k < len(messages) and messages[k][1] > place:
                places.append(place)
        return places

    def table(self):
        rows = np.tile(
            self.spare + np.arange(2 * self.count, dtype=np.int32), (self.slices, self.steps + 2, 1)
        )
        for z in range(self.slices):
            for step in range(self.steps + 2):
                for side, (messages, place) in enumerate(
                    ((self.right, z), (self.left, self.slices - 1 - z))
                ):
                    k = step - 2 * place
                    if 0 <= k < len(messages):
                        for b, square in enumerate(messages[k][0]):
                            rows[z, step, side * self.count + b] = square
        return rows.reshape(-1)

    def work_of(self, h, i, k, j):
        n = self.slices
        return self.work.index((self.calls.index((h, k)), 2 * j // n, 2 * i // n))

    def last_work(self, step):
        need = 0
        for messages in (self.right, self.left):
            for place in range(self.slices):
                k = step - 2 * place
                if 0 <= k < len(messages):
                    for square in messages[k][0]:
                        for (h, i, c, j), at in self.pair_at.items():
                            if at == square // 2:
                                need = max(need, self.work_of(h, i, c, j))
        return need

    def outputs(self):
        z_n, h_n = self.slices, self.parts
        ids = np.zeros((z_n, h_n, z_n, h_n, 2), np.int32)
        modes = np.zeros((z_n, h_n, z_n, h_n), np.int32)
        for z in range(z_n):
            for h in range(h_n):
                for j in range(z_n):
                    for k in range(h_n):
                        if (h, z, k, j) in self.pair_at:
                            ids[z, h, j, k] = self.squares(h, z, k, j)
                            modes[z, h, j, k] = 2 if (h, z) == (k, j) else 0
                        else:
                            ids[z, h, j, k] = self.squares(k, j, h, z)
                            modes[z, h, j, k] = 1
        return ids, modes


def hop_kernel(receives, sends, held, count, steps, step, tab, place, *refs):
    refs = list(refs)
    partial = refs.pop(0) if sends else None
    came = [refs.pop(0) for _ in range(2 if receives else 0)]
    outs = refs[held:]
    kept = [outs.pop(0) for _ in range(2 if receives else 0)]
    sent = [outs.pop(0) for _ in range(2 if sends else 0)]
    own = outs.pop(0) if sends else None
    sems = outs.pop(0)
    at = (place[0] * steps + step) * 2 * count
    slots = [(side, b) for side in range(2) for b in range(count)]
    loads, stores = [], []
    for side, b in slots:
        square = tab[at + side * count + b]
        if sends:
            loads.append(
                pltpu.make_async_copy(partial.at[square], own.at[side, b], sems.at[0, side, b])
            )
            loads[-1].start()
        if receives:
            stores.append(
                pltpu.make_async_copy(came[side].at[b], kept[side].at[square], sems.at[1, side, b])
            )
            stores[-1].start()
    if sends:
        for load, (side, b) in zip(loads, slots):
            load.wait()
            total = own[side, b]
            if receives:
                total = total + came[side][b].astype(F32)
            sent[side][b] = total.astype(BF16)
    for store in stores:
        store.wait()


def hop(table, place, steps, step, count, partial, received, kept, sends, after):
    size = partial.shape[1]
    inside = pl.BlockSpec(memory_space=pltpu.VMEM)
    anywhere = pl.BlockSpec(memory_space=pl.ANY)
    numbers = pl.BlockSpec(memory_space=pltpu.SMEM)
    receives = received is not None
    message = jax.ShapeDtypeStruct((count, size, size), BF16)
    in_specs, operands = [numbers, numbers], [table, place]
    out_specs, out_shape, aliases = [], [], {}
    if sends:
        in_specs += [anywhere]
        operands += [partial]
    if receives:
        aliases = {len(operands) + 2: 0, len(operands) + 3: 1}
        in_specs += [inside, inside, anywhere, anywhere]
        operands += [*received, *kept]
        out_specs += [anywhere, anywhere]
        out_shape += [jax.ShapeDtypeStruct(k.shape, k.dtype) for k in kept]
    in_specs += [anywhere] * len(after)
    operands += after
    scratch = []
    if sends:
        out_specs += [inside, inside]
        out_shape += [message, message]
        scratch = [pltpu.VMEM((2, count, size, size), F32)]
    found = pl.pallas_call(
        functools.partial(
            hop_kernel, receives, sends, (2 if receives else 0) + len(after), count, steps, step
        ),
        in_specs=in_specs,
        out_specs=out_specs,
        out_shape=out_shape,
        scratch_shapes=scratch + [pltpu.SemaphoreType.DMA((2, 2, count))],
        input_output_aliases=aliases,
        compiler_params=params(46 * 1024 * 1024),
        cost_estimate=pl.CostEstimate(
            flops=4 * count * size * size, bytes_accessed=20 * count * size * size, transcendentals=0
        ),
        name="hop",
    )(*operands)
    if receives:
        kept, found = found[:2], found[2:]
    return kept, (found if sends else None)


def piece(slices, parts, early, z, step):
    high = lax.div(2 * z, jnp.int32(slices))
    if not early:
        return parts - 1, high
    return lax.rem(step, jnp.int32(parts)), jnp.where(step < parts, 1 - high, high)


def rows_kernel(slices, parts, span, part, local, early, tab, mode, place, *refs):
    n = slices // 2 * parts * 2
    own, right, left = refs[:n], refs[n : 2 * n], refs[2 * n : 3 * n]
    tiles = refs[-1].shape[4]
    out_ref = refs[-1].reshape(span * part * 2 * tiles, LANES)
    z = place[0]
    h, half = piece(slices, parts, early, z, pl.program_id(0))
    first = half * (slices // 2)
    has_right, has_left = z > 0, z < slices - 1
    size = span * part

    def total(at):
        r = jnp.where(has_right, right[at][0].astype(F32), 0.0)
        l = jnp.where(has_left, left[at][0].astype(F32), 0.0)
        return own[at][0] + r + l

    for j in range(slices // 2):
        for k in range(parts):
            at = 2 * (j * parts + k)
            kind = mode[((z * parts + h) * slices + first + j) * parts + k]

            def put(ri, value, j=j, k=k):
                for d in range(span):
                    for e in range(span):
                        tile = (d * part * 2 + ri) * tiles + ((j * span + e) * local + k * part) // LANES
                        out_ref[pl.ds(tile, part, stride=2 * tiles), :] = value[
                            d * part : (d + 1) * part, e * part : (e + 1) * part
                        ]

            @pl.when(kind == 0)
            def _():
                put(0, total(at))
                put(1, total(at + 1))

            @pl.when(kind == 1)
            def _():
                put(0, total(at).T)
                put(1, -(total(at + 1).T))

            @pl.when(kind == 2)
            def _():
                direct = total(at)
                mirror = direct.T
                row = lax.broadcasted_iota(jnp.int32, (size, size), 0)
                col = lax.broadcasted_iota(jnp.int32, (size, size), 1)
                put(0, jnp.where(row >= col, direct, mirror))
                put(1, jnp.where(row < col, direct, jnp.where(row == col, 0.0, -mirror)))


def visibility_rows(plan, place, partial, kept, span, part, antennas, out):
    slices, parts = plan.slices, plan.parts
    size = span * part
    local = parts * part
    ids, modes = plan.outputs()
    early = out is None
    per_j = parts * 2
    per_half = slices // 2 * per_j

    def start(s, place):
        h, half = piece(slices, parts, early, place[0], s)
        return 2 * (place[0] * parts + h) + half

    def out_map(s, tab, mode, place):
        h, half = piece(slices, parts, early, place[0], s)
        return 0, h, 0, half, 0, 0

    def spec(at):
        return pl.BlockSpec(
            (1, size, size),
            lambda s, tab, mode, place: (tab[start(s, place) * per_half + at], 0, 0),
        )

    tiles = antennas // 2 // LANES
    again = [] if out is None else [out]
    operands = [partial] * per_half + [kept[0]] * per_half + [kept[1]] * per_half + again
    return pl.pallas_call(
        functools.partial(rows_kernel, slices, parts, span, part, local, early),
        grid_spec=pltpu.PrefetchScalarGridSpec(
            num_scalar_prefetch=3,
            grid=(2 * parts - 1 if early else 1,),
            in_specs=[spec(at) for _ in range(3) for at in range(per_half)]
            + [pl.BlockSpec(memory_space=pl.ANY) for _ in again],
            out_specs=pl.BlockSpec(
                (span, 1, part * 2, 1, tiles, LANES), out_map
            ),
        ),
        out_shape=jax.ShapeDtypeStruct((span, parts, part * 2, 2, tiles, LANES), F32),
        input_output_aliases={} if out is None else {3 + 3 * per_half: 0},
        compiler_params=params(),
        cost_estimate=pl.CostEstimate(
            flops=span * local * antennas * 4,
            bytes_accessed=span * local * antennas * 12,
            transcendentals=0,
        ),
        name="visibility_rows",
    )(jnp.asarray(ids.reshape(-1)), jnp.asarray(modes.reshape(-1)), place, *operands)


def on_device(voltages, filter_taps, antenna_flags):
    taps, length = filter_taps.shape
    channels, slices = lax.axis_size("chan"), lax.axis_size("tm")
    local = voltages.shape[1]
    samples = voltages.shape[2]
    frames = samples // length
    part = 128
    parts = local // part
    span = channels // slices

    head = taps * length
    halos = []
    for h in range(parts):
        tail = voltages[:, h * part : (h + 1) * part, samples - head :]
        halos.append(lax.ppermute(tail, "tm", [(i, i + 1) for i in range(slices - 1)]))
    weights = filterbank_weights(filter_taps, channels)
    scale = antenna_flags.reshape(1, local)

    plan = Plan(slices, parts, 4)
    table = jnp.asarray(plan.table())
    place = lax.axis_index("tm").astype(jnp.int32).reshape(1)
    weight = 1.0 / (frames * slices)
    antennas = channels * local
    spectra, token = [], weights
    for h in range(parts):
        pieces = 2 if h == 0 else 1
        chunk = frames // pieces
        found = []
        for t in reversed(range(pieces)):
            own, token = filterbank(
                voltages, halos[h], weights, scale, length, channels, part, h, t * chunk, chunk, token
            )
            found.insert(
                0, lax.all_to_all(own, "chan", split_axis=0, concat_axis=0, tiled=True)
            )
        spectra.append(found)

    done = []

    def extend(partial, kept, count):
        for _ in range(count):
            call, which, upper = plan.work[len(done)]
            h, k = plan.calls[call]
            made = correlate(
                partial, plan.total, slices, call, spectra[h], spectra[k], span, weight, h == k,
                which, upper,
            )
            partial = made[0]
            if kept is None:
                kept = made[1:]
            done.append(call)
        return partial, kept

    def needed(step):
        must = max(0, plan.last_work(step) + 1 - len(done))
        soon = len(done) < len(plan.work) and len(done) <= plan.last_work(step + 1)
        early = soon and step != 0 and (plan.work[len(done)][0] == 0 or step > 3)
        return max(must, 1 if early else 0)

    partial, kept = None, None
    arrived, out = {}, None
    early = max(plan.first_ready(), plan.steps - 1)
    holds = []
    for step in range(plan.steps + 2):
        partial, kept = extend(partial, kept, needed(step))
        sends = step < plan.steps
        received = arrived.pop(step - 2, None)
        kept, outgoing = hop(
            table, place, plan.steps + 2, step, plan.count, partial, received, kept, sends, holds
        )
        holds = []
        if sends:
            right = [(p, p + 1) for p in plan.senders(plan.right, step)]
            end = slices - 1
            left = [(end - p, end - p - 1) for p in plan.senders(plan.left, step)]
            arrived[step] = [
                lax.ppermute(outgoing[0], "tm", right),
                lax.ppermute(outgoing[1], "tm", left),
            ]
        if step == early:
            out = visibility_rows(plan, place, partial, kept, span, part, antennas, None)
            holds = [out]
    out = visibility_rows(plan, place, partial, kept, span, part, antennas, out)
    return out.reshape(span * local, 2, 1, antennas)


def solution(mesh):
    placed = (P(None, "chan", "tm"), P(), P("chan"))
    return jax.shard_map(
        on_device,
        mesh=mesh,
        in_specs=placed,
        out_specs=P("tm", None, "chan", None),
        check_vma=False,
    )
```

```python
import functools
import math

import jax
import jax.numpy as jnp
import numpy as np
from jax import lax
from jax.experimental import pallas as pl
from jax.experimental.pallas import tpu as pltpu
from jax.sharding import PartitionSpec as P

F32, BF16 = jnp.float32, jnp.bfloat16
GROUP = 8
LANES = 128
FRAMES_PER_STEP = 128
VMEM_LIMIT = 52 * 1024 * 1024


def params(limit=VMEM_LIMIT):
    return pltpu.CompilerParams(vmem_limit_bytes=limit)


def weights_kernel(taps_ref, trig_ref, out_ref, wide):
    taps, length = taps_ref.shape
    rows = trig_ref.shape[0]
    size = GROUP * length
    flat = jnp.concatenate([taps_ref[taps - 1 - k : taps - k, :] for k in range(taps)], axis=1)
    base = flat * jnp.concatenate([trig_ref[...]] * taps, axis=1)
    for f in range(GROUP):
        before = jnp.zeros((rows, (f + 1) * length), F32)
        moved = [before, base]
        if f < GROUP - 1:
            moved.append(jnp.zeros((rows, (GROUP - 1 - f) * length), F32))
        moved = jnp.concatenate(moved, axis=1)
        for t in range(wide.shape[0]):
            wide[t, pl.ds(f, rows, stride=GROUP), :] = moved[:, t * LANES : (t + 1) * LANES]
    n = rows * GROUP
    each = size // LANES
    for t in range(wide.shape[0]):
        full = wide[t]
        high = full.astype(BF16).astype(F32)
        m, lanes = t // each, slice(t % each * LANES, (t % each + 1) * LANES)
        both = jnp.concatenate([high, full - high], axis=0).astype(BF16)
        out_ref[2 * m * n : 2 * (m + 1) * n, lanes] = both


def filterbank_weights(filter_taps, channels):
    taps, length = filter_taps.shape
    phase = np.arange(length)[None, :] * np.arange(channels)[:, None] % length
    angle = phase * (2.0 * math.pi / length)
    trig = np.stack([np.cos(angle), np.sin(angle)]).reshape(2 * channels, length)
    trig = np.delete(trig, channels, axis=0)
    rows = trig.shape[0] * GROUP
    blocks = taps // GROUP + 1
    return pl.pallas_call(
        weights_kernel,
        out_shape=jax.ShapeDtypeStruct((blocks * 2 * rows, GROUP * length), BF16),
        scratch_shapes=[pltpu.VMEM((blocks * GROUP * length // LANES, rows, LANES), F32)],
        compiler_params=params(),
        name="weights",
    )(filter_taps, jnp.asarray(trig.astype(np.float32)))


def filterbank_kernel(channels, length, head_ref, v_ref, w_ref, s_ref, after_ref, out_ref, token_ref, carry, found):
    del after_ref, token_ref
    step = pl.program_id(0)
    _, part, lanes = v_ref.shape
    size = GROUP * length
    half = channels * GROUP
    rows = carry.shape[1]
    blocks = w_ref.shape[0] // (2 * rows)
    scale = s_ref[...].astype(F32) / math.sqrt(length)

    def advance(ref, at):
        x = ref[:, :, at * size : (at + 1) * size].reshape(2 * part, size)
        r = lax.dot_general(w_ref[...], x, (((1,), (1,)), ((), ())), preferred_element_type=F32)
        third = [
            r[2 * m * rows : (2 * m + 1) * rows] + r[(2 * m + 1) * rows : (2 * m + 2) * rows]
            for m in range(blocks)
        ]
        done = carry[blocks - 2] + third[blocks - 1]
        for m in range(blocks - 2, 0, -1):
            carry[m] = carry[m - 1] + third[m]
        carry[0] = third[0]
        return done

    @pl.when(step == 0)
    def _():
        carry[...] = jnp.zeros_like(carry)
        for b in range(head_ref.shape[2] // size):
            advance(head_ref, b)

    for b in range(lanes // size):
        done = advance(v_ref, b)
        cos, sin = done[:half], done[half:]
        for c in range(channels):
            at = slice(c * GROUP, (c + 1) * GROUP)
            real, imag = cos[at, :part], cos[at, part:]
            if c > 0:
                at = slice((c - 1) * GROUP, c * GROUP)
                real, imag = real + sin[at, part:], imag - sin[at, :part]
            found[c, 0, b * GROUP : (b + 1) * GROUP, :] = real * scale
            found[c, 1, b * GROUP : (b + 1) * GROUP, :] = imag * scale
    for c in range(channels):
        for ri in range(2):
            out_ref[c, ri] = found[c, ri].T.astype(BF16)


def filterbank(voltages, halo, weights, scale, length, channels, part, h, start, frames, after):
    block = min(frames, FRAMES_PER_STEP)
    lanes = block * length
    head = halo.shape[2]
    first = start * length
    if start == 0:
        before, head_map = halo, lambda s: (0, 0, 0)
    else:
        before, head_map = voltages, lambda s: (0, h, first // head - 1)
    blocks = head // (GROUP * length)
    return pl.pallas_call(
        functools.partial(filterbank_kernel, channels, length),
        grid=(frames // block,),
        in_specs=[
            pl.BlockSpec((2, part, head), head_map),
            pl.BlockSpec((2, part, lanes), lambda s: (0, h, first // lanes + s)),
            pl.BlockSpec(weights.shape, lambda s: (0, 0)),
            pl.BlockSpec((1, part), lambda s: (0, h)),
            pl.BlockSpec(memory_space=pl.ANY),
        ],
        out_specs=[
            pl.BlockSpec((channels, 2, part, block), lambda s: (0, 0, 0, s)),
            pl.BlockSpec(memory_space=pl.ANY),
        ],
        out_shape=[
            jax.ShapeDtypeStruct((channels, 2, part, frames), BF16),
            jax.ShapeDtypeStruct((8, LANES), F32),
        ],
        scratch_shapes=[
            pltpu.VMEM((blocks, (2 * channels - 1) * GROUP, 2 * part), F32),
            pltpu.VMEM((channels, 2, block, part), F32),
        ],
        compiler_params=params(),
        cost_estimate=pl.CostEstimate(
            flops=2 * weights.size * 2 * part * frames // GROUP,
            bytes_accessed=2 * 2 * part * frames * length,
            transcendentals=0,
        ),
        name=f"filterbank_h{h}_f{start}",
    )(before, voltages, weights, scale, after)


def correlate_kernel(times, span, weight, fresh, same, low, first, *refs):
    xs, ys = refs[:times[0]], refs[times[0] : sum(times)]
    out_ref = refs[sum(times)] if fresh else refs[sum(times) + 1]
    part = xs[0].shape[2]
    size = span * part
    group = ys[0].shape[0] // span
    many = xs[0].shape[0] // span

    def side(some, start, count, ri):
        wide = [
            jnp.concatenate([ref[start + d, ri] for d in range(count)], axis=0) for ref in some
        ]
        return wide[0] if len(wide) == 1 else jnp.concatenate(wide, axis=1)

    on_real, on_imag = [], []
    for n in range(many):
        real, imag = side(xs, n * span, span, 0), side(xs, n * span, span, 1)
        on_real += [real, imag]
        on_imag += [imag, -real]
    turned = jnp.concatenate(
        [jnp.concatenate(on_real, axis=0), jnp.concatenate(on_imag, axis=0)], axis=1
    )
    other = [side(ys, 0, group * span, ri) for ri in range(2)]
    both = lax.dot_general(
        turned,
        jnp.concatenate(other, axis=1),
        (((1,), (1,)), ((), ())),
        preferred_element_type=F32,
    )
    both = (both * weight).astype(BF16)
    for m in range(many):
        i = pl.program_id(0) * many + low + m
        real = both[2 * m * size : (2 * m + 1) * size]
        imag = both[(2 * m + 1) * size : (2 * m + 2) * size]
        for n in range(group):
            columns = slice(n * size, (n + 1) * size)
            out_ref[m, 2 * n] = real[:, columns]
            out_ref[m, 2 * n + 1] = imag[:, columns]
            if same:

                @pl.when(i == first + n)
                def _():
                    row = lax.broadcasted_iota(jnp.int32, (size, size), 0)
                    col = lax.broadcasted_iota(jnp.int32, (size, size), 1)
                    out_ref[m, 2 * n] = jnp.where(row >= col, real[:, columns], imag[:, columns])


def correlate(partial, total, slices, call, xs, ys, span, weight, same, which, upper):
    part = xs[0].shape[2]
    size = span * part
    frames = sum(x.shape[3] for x in xs)
    group = slices // 2
    low = upper * group
    many = 1
    rows = [
        pl.BlockSpec((many * span, 2, part, x.shape[3]), lambda i: (low // many + i, 0, 0, 0))
        for x in xs
    ]
    columns = [
        pl.BlockSpec((group * span, 2, part, y.shape[3]), lambda i: (which, 0, 0, 0)) for y in ys
    ]
    out_block = pl.BlockSpec(
        (many, 2 * group, size, size), lambda i: ((call * slices + low) // many + i, which, 0, 0)
    )
    lines = total // (2 * slices)
    shape = jax.ShapeDtypeStruct((lines, 2 * slices, size, size), BF16)
    store = jax.ShapeDtypeStruct((total, size, size), BF16)
    fresh = partial is None
    if not fresh:
        partial = partial.reshape(shape.shape)
    anywhere = pl.BlockSpec(memory_space=pl.ANY)
    made = pl.pallas_call(
        functools.partial(
            correlate_kernel, (len(xs), len(ys)), span, weight, fresh, same, low, which * group
        ),
        grid=(group // many,),
        in_specs=rows + columns + ([] if fresh else [anywhere]),
        out_specs=[out_block, anywhere, anywhere] if fresh else [out_block],
        out_shape=[shape, store, store] if fresh else [shape],
        input_output_aliases={} if fresh else {len(xs) + len(ys): 0},
        compiler_params=params(),
        cost_estimate=pl.CostEstimate(
            flops=8 * group * group * size * size * frames,
            bytes_accessed=8 * group * group * size * size,
            transcendentals=0,
        ),
        name="correlate",
    )(*xs, *ys, *([] if fresh else [partial]))
    return [made[0].reshape(total, size, size)] + list(made[1:])


class Plan:
    def __init__(self, slices, parts, count):
        self.slices, self.parts, self.count = slices, parts, count
        self.calls = []
        self.pair_at = {}
        for h in range(parts):
            for k in range(h, -1, -1):
                first = len(self.calls) * slices * slices
                self.calls.append((h, k))
                for i in range(slices):
                    for j in range(slices):
                        if k < h or j <= i:
                            self.pair_at[h, i, k, j] = first + i * slices + j
        self.work = []
        for call, (h, k) in enumerate(self.calls):
            quarters = [(0, 1), (0, 0), (1, 1)] if h == k else [(0, 1), (1, 0), (1, 1), (0, 0)]
            self.work += [(call, which, upper) for which, upper in quarters]
        self.spare = 2 * len(self.calls) * slices * slices
        self.total = self.spare + -(-2 * count // (2 * slices)) * 2 * slices
        self.right = self.messages(lambda i, j: max(i, j))
        self.left = self.messages(lambda i, j: slices - 1 - min(i, j))
        self.steps = 0
        for index in range(2 * (len(self.right) + len(self.left)) + 4 * slices):
            if self.senders(self.right, index) or self.senders(self.left, index):
                self.steps = index + 1

    def squares(self, h, i, k, j):
        at = 2 * self.pair_at[h, i, k, j]
        return (at, at) if (h, i) == (k, j) else (at, at + 1)

    def messages(self, reach):
        slices = self.slices
        queues, last = [[] for _ in self.calls], []
        for (h, i, k, j) in self.pair_at:
            far = reach(i, j)
            if far:
                late = self.late(i, j) and self.late(j, i)
                for square in sorted(set(self.squares(h, i, k, j))):
                    if far == 1:
                        late = self.only_last(h, i, k, j)
                    order = (-far, late, self.work_of(h, i, k, j))
                    if far > 1 and h == k:
                        order = (order[2],) + order[:2]
                    elif far > 1:
                        first = self.work_of(self.calls[-1][0], slices - 1, self.calls[-1][1], 0)
                        if far == slices - 1:
                            after = late and self.ends_last(h, i, k, j, reach)
                            order = (2 if late else 0, after, order[2])
                        elif order[2] == first and not late:
                            order = (1, False, order[2])
                        else:
                            order = (2 + slices - far, late, order[2])
                    entry = order + (far, square)
                    (queues[self.calls.index((h, k))] if far > 1 else last).append(entry)
        if self.slices == 2:
            queues, last = [last], []
        found = []
        for queue in [sorted(q) for q in queues] + [sorted(last)]:
            for at in range(0, len(queue), self.count):
                some = queue[at : at + self.count]
                ids = [entry[-1] for entry in some]
                found.append((ids, max(entry[-2] for entry in some)))
        return found

    def late(self, z, j):
        return (2 * z < self.slices) == (2 * j < self.slices)

    def only_last(self, h, i, k, j):
        near = (1, self.slices - 2)
        touched = [part for part, z in ((h, i), (k, j)) if z in near]
        return all(part == self.parts - 1 for part in touched)

    def ends_last(self, h, i, k, j, reach):
        end = self.slices - 1 if reach(self.slices - 1, 0) > reach(0, 0) else 0
        touched = [part for part, z in ((h, i), (k, j)) if z == end]
        return all(part == self.parts - 1 for part in touched)

    def first_ready(self):
        ready = 0
        ids, _ = self.outputs()
        for z in range(self.slices):
            for messages, place in ((self.right, z), (self.left, self.slices - 1 - z)):
                if place == 0:
                    continue
                for k, (squares, _) in enumerate(messages):
                    for j in range(self.slices):
                        parts = self.parts - 1 if self.late(z, j) else self.parts
                        if set(ids[z, :parts, j].ravel()) & set(squares):
                            ready = max(ready, k + 2 * place)
        return ready

    def senders(self, messages, step):
        places = []
        for place in range(self.slices - 1):
            k = step - 2 * place
            if 0 <= k < len(messages) and messages[k][1] > place:
                places.append(place)
        return places

    def table(self):
        rows = np.tile(
            self.spare + np.arange(2 * self.count, dtype=np.int32), (self.slices, self.steps + 2, 1)
        )
        for z in range(self.slices):
            for step in range(self.steps + 2):
                for side, (messages, place) in enumerate(
                    ((self.right, z), (self.left, self.slices - 1 - z))
                ):
                    k = step - 2 * place
                    if 0 <= k < len(messages):
                        for b, square in enumerate(messages[k][0]):
                            rows[z, step, side * self.count + b] = square
        return rows.reshape(-1)

    def work_of(self, h, i, k, j):
        n = self.slices
        return self.work.index((self.calls.index((h, k)), 2 * j // n, 2 * i // n))

    def last_work(self, step):
        need = 0
        for messages in (self.right, self.left):
            for place in range(self.slices):
                k = step - 2 * place
                if 0 <= k < len(messages):
                    for square in messages[k][0]:
                        for (h, i, c, j), at in self.pair_at.items():
                            if at == square // 2:
                                need = max(need, self.work_of(h, i, c, j))
        return need

    def outputs(self):
        z_n, h_n = self.slices, self.parts
        ids = np.zeros((z_n, h_n, z_n, h_n, 2), np.int32)
        modes = np.zeros((z_n, h_n, z_n, h_n), np.int32)
        for z in range(z_n):
            for h in range(h_n):
                for j in range(z_n):
                    for k in range(h_n):
                        if (h, z, k, j) in self.pair_at:
                            ids[z, h, j, k] = self.squares(h, z, k, j)
                            modes[z, h, j, k] = 2 if (h, z) == (k, j) else 0
                        else:
                            ids[z, h, j, k] = self.squares(k, j, h, z)
                            modes[z, h, j, k] = 1
        return ids, modes


def hop_kernel(receives, sends, held, count, steps, step, tab, place, *refs):
    refs = list(refs)
    partial = refs.pop(0) if sends else None
    came = [refs.pop(0) for _ in range(2 if receives else 0)]
    outs = refs[held:]
    kept = [outs.pop(0) for _ in range(2 if receives else 0)]
    sent = [outs.pop(0) for _ in range(2 if sends else 0)]
    own = outs.pop(0) if sends else None
    sems = outs.pop(0)
    at = (place[0] * steps + step) * 2 * count
    slots = [(side, b) for side in range(2) for b in range(count)]
    loads, stores = [], []
    for side, b in slots:
        square = tab[at + side * count + b]
        if sends:
            loads.append(
                pltpu.make_async_copy(partial.at[square], own.at[side, b], sems.at[0, side, b])
            )
            loads[-1].start()
        if receives:
            stores.append(
                pltpu.make_async_copy(came[side].at[b], kept[side].at[square], sems.at[1, side, b])
            )
            stores[-1].start()
    if sends:
        for load, (side, b) in zip(loads, slots):
            load.wait()
            total = own[side, b]
            if receives:
                total = (total.astype(F32) + came[side][b].astype(F32)).astype(BF16)
            sent[side][b] = total
    for store in stores:
        store.wait()


def hop(table, place, steps, step, count, partial, received, kept, sends, after):
    size = partial.shape[1]
    inside = pl.BlockSpec(memory_space=pltpu.VMEM)
    anywhere = pl.BlockSpec(memory_space=pl.ANY)
    numbers = pl.BlockSpec(memory_space=pltpu.SMEM)
    receives = received is not None
    message = jax.ShapeDtypeStruct((count, size, size), BF16)
    in_specs, operands = [numbers, numbers], [table, place]
    out_specs, out_shape, aliases = [], [], {}
    if sends:
        in_specs += [anywhere]
        operands += [partial]
    if receives:
        aliases = {len(operands) + 2: 0, len(operands) + 3: 1}
        in_specs += [inside, inside, anywhere, anywhere]
        operands += [*received, *kept]
        out_specs += [anywhere, anywhere]
        out_shape += [jax.ShapeDtypeStruct(k.shape, k.dtype) for k in kept]
    in_specs += [anywhere] * len(after)
    operands += after
    scratch = []
    if sends:
        out_specs += [inside, inside]
        out_shape += [message, message]
        scratch = [pltpu.VMEM((2, count, size, size), BF16)]
    found = pl.pallas_call(
        functools.partial(
            hop_kernel, receives, sends, (2 if receives else 0) + len(after), count, steps, step
        ),
        in_specs=in_specs,
        out_specs=out_specs,
        out_shape=out_shape,
        scratch_shapes=scratch + [pltpu.SemaphoreType.DMA((2, 2, count))],
        input_output_aliases=aliases,
        compiler_params=params(46 * 1024 * 1024),
        cost_estimate=pl.CostEstimate(
            flops=4 * count * size * size, bytes_accessed=20 * count * size * size, transcendentals=0
        ),
        name="hop",
    )(*operands)
    if receives:
        kept, found = found[:2], found[2:]
    return kept, (found if sends else None)


def piece(slices, parts, early, z, step):
    high = lax.div(2 * z, jnp.int32(slices))
    if not early:
        return parts - 1, high
    return lax.rem(step, jnp.int32(parts)), jnp.where(step < parts, 1 - high, high)


def rows_kernel(slices, parts, span, part, local, early, tab, mode, place, *refs):
    n = slices // 2 * parts * 2
    own, right, left = refs[:n], refs[n : 2 * n], refs[2 * n : 3 * n]
    tiles = refs[-1].shape[4]
    out_ref = refs[-1].reshape(span * part * 2 * tiles, LANES)
    z = place[0]
    h, half = piece(slices, parts, early, z, pl.program_id(0))
    first = half * (slices // 2)
    has_right, has_left = z > 0, z < slices - 1
    size = span * part

    def total(at):
        r = jnp.where(has_right, right[at][0].astype(F32), 0.0)
        l = jnp.where(has_left, left[at][0].astype(F32), 0.0)
        return own[at][0].astype(F32) + r + l

    for j in range(slices // 2):
        for k in range(parts):
            at = 2 * (j * parts + k)
            kind = mode[((z * parts + h) * slices + first + j) * parts + k]

            def put(ri, value, j=j, k=k):
                for d in range(span):
                    for e in range(span):
                        tile = (d * part * 2 + ri) * tiles + ((j * span + e) * local + k * part) // LANES
                        out_ref[pl.ds(tile, part, stride=2 * tiles), :] = value[
                            d * part : (d + 1) * part, e * part : (e + 1) * part
                        ]

            @pl.when(kind == 0)
            def _():
                put(0, total(at))
                put(1, total(at + 1))

            @pl.when(kind == 1)
            def _():
                put(0, total(at).T)
                put(1, -(total(at + 1).T))

            @pl.when(kind == 2)
            def _():
                direct = total(at)
                mirror = direct.T
                row = lax.broadcasted_iota(jnp.int32, (size, size), 0)
                col = lax.broadcasted_iota(jnp.int32, (size, size), 1)
                put(0, jnp.where(row >= col, direct, mirror))
                put(1, jnp.where(row < col, direct, jnp.where(row == col, 0.0, -mirror)))


def visibility_rows(plan, place, partial, kept, span, part, antennas, out):
    slices, parts = plan.slices, plan.parts
    size = span * part
    local = parts * part
    ids, modes = plan.outputs()
    early = out is None
    per_j = parts * 2
    per_half = slices // 2 * per_j

    def start(s, place):
        h, half = piece(slices, parts, early, place[0], s)
        return 2 * (place[0] * parts + h) + half

    def out_map(s, tab, mode, place):
        h, half = piece(slices, parts, early, place[0], s)
        return 0, h, 0, half, 0, 0

    def spec(at):
        return pl.BlockSpec(
            (1, size, size),
            lambda s, tab, mode, place: (tab[start(s, place) * per_half + at], 0, 0),
        )

    tiles = antennas // 2 // LANES
    again = [] if out is None else [out]
    operands = [partial] * per_half + [kept[0]] * per_half + [kept[1]] * per_half + again
    return pl.pallas_call(
        functools.partial(rows_kernel, slices, parts, span, part, local, early),
        grid_spec=pltpu.PrefetchScalarGridSpec(
            num_scalar_prefetch=3,
            grid=(2 * parts - 1 if early else 1,),
            in_specs=[spec(at) for _ in range(3) for at in range(per_half)]
            + [pl.BlockSpec(memory_space=pl.ANY) for _ in again],
            out_specs=pl.BlockSpec(
                (span, 1, part * 2, 1, tiles, LANES), out_map
            ),
        ),
        out_shape=jax.ShapeDtypeStruct((span, parts, part * 2, 2, tiles, LANES), F32),
        input_output_aliases={} if out is None else {3 + 3 * per_half: 0},
        compiler_params=params(),
        cost_estimate=pl.CostEstimate(
            flops=span * local * antennas * 4,
            bytes_accessed=span * local * antennas * 12,
            transcendentals=0,
        ),
        name="visibility_rows",
    )(jnp.asarray(ids.reshape(-1)), jnp.asarray(modes.reshape(-1)), place, *operands)


def on_device(voltages, filter_taps, antenna_flags):
    taps, length = filter_taps.shape
    channels, slices = lax.axis_size("chan"), lax.axis_size("tm")
    local = voltages.shape[1]
    samples = voltages.shape[2]
    frames = samples // length
    part = 128
    parts = local // part
    span = channels // slices

    head = taps * length
    halos = []
    for h in range(parts):
        tail = voltages[:, h * part : (h + 1) * part, samples - head :]
        halos.append(lax.ppermute(tail, "tm", [(i, i + 1) for i in range(slices - 1)]))
    weights = filterbank_weights(filter_taps, channels)
    scale = antenna_flags.reshape(1, local)

    plan = Plan(slices, parts, 4)
    table = jnp.asarray(plan.table())
    place = lax.axis_index("tm").astype(jnp.int32).reshape(1)
    weight = 1.0 / (frames * slices)
    antennas = channels * local
    spectra, token = [], weights
    for h in range(parts):
        pieces = 2 if h == 0 else 1
        chunk = frames // pieces
        found = []
        for t in reversed(range(pieces)):
            own, token = filterbank(
                voltages, halos[h], weights, scale, length, channels, part, h, t * chunk, chunk, token
            )
            found.insert(
                0, lax.all_to_all(own, "chan", split_axis=0, concat_axis=0, tiled=True)
            )
        spectra.append(found)

    done = []

    def extend(partial, kept, count):
        for _ in range(count):
            call, which, upper = plan.work[len(done)]
            h, k = plan.calls[call]
            made = correlate(
                partial, plan.total, slices, call, spectra[h], spectra[k], span, weight, h == k,
                which, upper,
            )
            partial = made[0]
            if kept is None:
                kept = made[1:]
            done.append(call)
        return partial, kept

    def needed(step):
        must = max(0, plan.last_work(step) + 1 - len(done))
        soon = len(done) < len(plan.work) and len(done) <= plan.last_work(step + 1)
        early = soon and step != 0 and (plan.work[len(done)][0] == 0 or step > 3)
        return max(must, 1 if early else 0)

    partial, kept = None, None
    arrived, out = {}, None
    early = max(plan.first_ready(), plan.steps - 1)
    holds = []
    for step in range(plan.steps + 2):
        partial, kept = extend(partial, kept, needed(step))
        sends = step < plan.steps
        received = arrived.pop(step - 2, None)
        kept, outgoing = hop(
            table, place, plan.steps + 2, step, plan.count, partial, received, kept, sends, holds
        )
        holds = []
        if sends:
            right = [(p, p + 1) for p in plan.senders(plan.right, step)]
            end = slices - 1
            left = [(end - p, end - p - 1) for p in plan.senders(plan.left, step)]
            arrived[step] = [
                lax.ppermute(outgoing[0], "tm", right),
                lax.ppermute(outgoing[1], "tm", left),
            ]
        if step == early:
            out = visibility_rows(plan, place, partial, kept, span, part, antennas, None)
            holds = [out]
    out = visibility_rows(plan, place, partial, kept, span, part, antennas, out)
    return out.reshape(span * local, 2, 1, antennas)


def solution(mesh):
    placed = (P(None, "chan", "tm"), P(), P("chan"))
    return jax.shard_map(
        on_device,
        mesh=mesh,
        in_specs=placed,
        out_specs=P("tm", None, "chan", None),
        check_vma=False,
    )
```

```python
import functools
import math

import jax
import jax.numpy as jnp
import numpy as np
from jax import lax
from jax.experimental import pallas as pl
from jax.experimental.pallas import tpu as pltpu
from jax.sharding import PartitionSpec as P

F32, BF16 = jnp.float32, jnp.bfloat16
GROUP = 8
LANES = 128
FRAMES_PER_STEP = 128
VMEM_LIMIT = 46 * 1024 * 1024


def params(limit=VMEM_LIMIT):
    return pltpu.CompilerParams(vmem_limit_bytes=limit)


def weights_kernel(taps_ref, trig_ref, out_ref, wide):
    taps, length = taps_ref.shape
    rows = trig_ref.shape[0]
    size = GROUP * length
    flat = jnp.concatenate([taps_ref[taps - 1 - k : taps - k, :] for k in range(taps)], axis=1)
    base = flat * jnp.concatenate([trig_ref[...]] * taps, axis=1)
    for f in range(GROUP):
        before = jnp.zeros((rows, (f + 1) * length), F32)
        moved = [before, base]
        if f < GROUP - 1:
            moved.append(jnp.zeros((rows, (GROUP - 1 - f) * length), F32))
        moved = jnp.concatenate(moved, axis=1)
        for t in range(wide.shape[0]):
            wide[t, pl.ds(f, rows, stride=GROUP), :] = moved[:, t * LANES : (t + 1) * LANES]
    n = rows * GROUP
    each = size // LANES
    for t in range(wide.shape[0]):
        full = wide[t]
        high = full.astype(BF16).astype(F32)
        m, lanes = t // each, slice(t % each * LANES, (t % each + 1) * LANES)
        both = jnp.concatenate([high, full - high], axis=0).astype(BF16)
        out_ref[2 * m * n : 2 * (m + 1) * n, lanes] = both


def filterbank_weights(filter_taps, channels):
    taps, length = filter_taps.shape
    phase = np.arange(length)[None, :] * np.arange(channels)[:, None] % length
    angle = phase * (2.0 * math.pi / length)
    trig = np.stack([np.cos(angle), np.sin(angle)]).reshape(2 * channels, length)
    trig = np.delete(trig, channels, axis=0)
    rows = trig.shape[0] * GROUP
    blocks = taps // GROUP + 1
    return pl.pallas_call(
        weights_kernel,
        out_shape=jax.ShapeDtypeStruct((blocks * 2 * rows, GROUP * length), BF16),
        scratch_shapes=[pltpu.VMEM((blocks * GROUP * length // LANES, rows, LANES), F32)],
        compiler_params=params(),
        name="weights",
    )(filter_taps, jnp.asarray(trig.astype(np.float32)))


def filterbank_kernel(channels, length, head_ref, v_ref, w_ref, s_ref, after_ref, out_ref, token_ref, carry, found):
    del after_ref, token_ref
    step = pl.program_id(0)
    _, part, lanes = v_ref.shape
    size = GROUP * length
    half = channels * GROUP
    rows = carry.shape[1]
    blocks = w_ref.shape[0] // (2 * rows)
    scale = s_ref[...].astype(F32) / math.sqrt(length)

    def advance(ref, at):
        x = ref[:, :, at * size : (at + 1) * size].reshape(2 * part, size)
        r = lax.dot_general(w_ref[...], x, (((1,), (1,)), ((), ())), preferred_element_type=F32)
        third = [
            r[2 * m * rows : (2 * m + 1) * rows] + r[(2 * m + 1) * rows : (2 * m + 2) * rows]
            for m in range(blocks)
        ]
        done = carry[blocks - 2] + third[blocks - 1]
        for m in range(blocks - 2, 0, -1):
            carry[m] = carry[m - 1] + third[m]
        carry[0] = third[0]
        return done

    @pl.when(step == 0)
    def _():
        carry[...] = jnp.zeros_like(carry)
        for b in range(head_ref.shape[2] // size):
            advance(head_ref, b)

    for b in range(lanes // size):
        done = advance(v_ref, b)
        cos, sin = done[:half], done[half:]
        for c in range(channels):
            at = slice(c * GROUP, (c + 1) * GROUP)
            real, imag = cos[at, :part], cos[at, part:]
            if c > 0:
                at = slice((c - 1) * GROUP, c * GROUP)
                real, imag = real + sin[at, part:], imag - sin[at, :part]
            found[c, 0, b * GROUP : (b + 1) * GROUP, :] = real * scale
            found[c, 1, b * GROUP : (b + 1) * GROUP, :] = imag * scale
    for c in range(channels):
        for ri in range(2):
            out_ref[c, ri] = found[c, ri].T.astype(BF16)


def filterbank(voltages, halo, weights, scale, length, channels, part, h, start, frames, after):
    block = min(frames, FRAMES_PER_STEP)
    lanes = block * length
    head = halo.shape[2]
    first = start * length
    if start == 0:
        before, head_map = halo, lambda s: (0, 0, 0)
    else:
        before, head_map = voltages, lambda s: (0, h, first // head - 1)
    blocks = head // (GROUP * length)
    return pl.pallas_call(
        functools.partial(filterbank_kernel, channels, length),
        grid=(frames // block,),
        in_specs=[
            pl.BlockSpec((2, part, head), head_map),
            pl.BlockSpec((2, part, lanes), lambda s: (0, h, first // lanes + s)),
            pl.BlockSpec(weights.shape, lambda s: (0, 0)),
            pl.BlockSpec((1, part), lambda s: (0, h)),
            pl.BlockSpec(memory_space=pl.ANY),
        ],
        out_specs=[
            pl.BlockSpec((channels, 2, part, block), lambda s: (0, 0, 0, s)),
            pl.BlockSpec(memory_space=pl.ANY),
        ],
        out_shape=[
            jax.ShapeDtypeStruct((channels, 2, part, frames), BF16),
            jax.ShapeDtypeStruct((8, LANES), F32),
        ],
        scratch_shapes=[
            pltpu.VMEM((blocks, (2 * channels - 1) * GROUP, 2 * part), F32),
            pltpu.VMEM((channels, 2, block, part), F32),
        ],
        compiler_params=params(),
        cost_estimate=pl.CostEstimate(
            flops=2 * weights.size * 2 * part * frames // GROUP,
            bytes_accessed=2 * 2 * part * frames * length,
            transcendentals=0,
        ),
        name=f"filterbank_h{h}_f{start}",
    )(before, voltages, weights, scale, after)


def correlate_kernel(times, span, weight, fresh, same, low, first, *refs):
    xs, ys = refs[:times[0]], refs[times[0] : sum(times)]
    out_ref = refs[sum(times)] if fresh else refs[sum(times) + 1]
    part = xs[0].shape[2]
    size = span * part
    group = ys[0].shape[0] // span
    many = xs[0].shape[0] // span

    def side(some, start, count, ri):
        wide = [
            jnp.concatenate([ref[start + d, ri] for d in range(count)], axis=0) for ref in some
        ]
        return wide[0] if len(wide) == 1 else jnp.concatenate(wide, axis=1)

    on_real, on_imag = [], []
    for n in range(many):
        real, imag = side(xs, n * span, span, 0), side(xs, n * span, span, 1)
        on_real += [real, imag]
        on_imag += [imag, -real]
    turned = jnp.concatenate(
        [jnp.concatenate(on_real, axis=0), jnp.concatenate(on_imag, axis=0)], axis=1
    )
    other = [side(ys, 0, group * span, ri) for ri in range(2)]
    both = lax.dot_general(
        turned,
        jnp.concatenate(other, axis=1),
        (((1,), (1,)), ((), ())),
        preferred_element_type=F32,
    )
    both = (both * weight).astype(BF16)
    for m in range(many):
        i = pl.program_id(0) * many + low + m
        real = both[2 * m * size : (2 * m + 1) * size]
        imag = both[(2 * m + 1) * size : (2 * m + 2) * size]
        for n in range(group):
            columns = slice(n * size, (n + 1) * size)
            out_ref[m, 2 * n] = real[:, columns]
            out_ref[m, 2 * n + 1] = imag[:, columns]
            if same:

                @pl.when(i == first + n)
                def _():
                    row = lax.broadcasted_iota(jnp.int32, (size, size), 0)
                    col = lax.broadcasted_iota(jnp.int32, (size, size), 1)
                    out_ref[m, 2 * n] = jnp.where(row >= col, real[:, columns], imag[:, columns])


def correlate(partial, total, slices, call, xs, ys, span, weight, same, which, upper):
    part = xs[0].shape[2]
    size = span * part
    frames = sum(x.shape[3] for x in xs)
    group = slices // 2
    low = upper * group
    many = 1
    rows = [
        pl.BlockSpec((many * span, 2, part, x.shape[3]), lambda i: (low // many + i, 0, 0, 0))
        for x in xs
    ]
    columns = [
        pl.BlockSpec((group * span, 2, part, y.shape[3]), lambda i: (which, 0, 0, 0)) for y in ys
    ]
    out_block = pl.BlockSpec(
        (many, 2 * group, size, size), lambda i: ((call * slices + low) // many + i, which, 0, 0)
    )
    lines = total // (2 * slices)
    shape = jax.ShapeDtypeStruct((lines, 2 * slices, size, size), BF16)
    store = jax.ShapeDtypeStruct((total, size, size), BF16)
    fresh = partial is None
    if not fresh:
        partial = partial.reshape(shape.shape)
    anywhere = pl.BlockSpec(memory_space=pl.ANY)
    made = pl.pallas_call(
        functools.partial(
            correlate_kernel, (len(xs), len(ys)), span, weight, fresh, same, low, which * group
        ),
        grid=(group // many,),
        in_specs=rows + columns + ([] if fresh else [anywhere]),
        out_specs=[out_block, anywhere, anywhere] if fresh else [out_block],
        out_shape=[shape, store, store] if fresh else [shape],
        input_output_aliases={} if fresh else {len(xs) + len(ys): 0},
        compiler_params=params(),
        cost_estimate=pl.CostEstimate(
            flops=8 * group * group * size * size * frames,
            bytes_accessed=8 * group * group * size * size,
            transcendentals=0,
        ),
        name="correlate",
    )(*xs, *ys, *([] if fresh else [partial]))
    return [made[0].reshape(total, size, size)] + list(made[1:])


class Plan:
    def __init__(self, slices, parts, count):
        self.slices, self.parts, self.count = slices, parts, count
        self.calls = []
        self.pair_at = {}
        for h in range(parts):
            for k in range(h, -1, -1):
                first = len(self.calls) * slices * slices
                self.calls.append((h, k))
                for i in range(slices):
                    for j in range(slices):
                        if k < h or j <= i:
                            self.pair_at[h, i, k, j] = first + i * slices + j
        self.work = []
        for call, (h, k) in enumerate(self.calls):
            quarters = [(0, 1), (0, 0), (1, 1)] if h == k else [(0, 1), (1, 0), (1, 1), (0, 0)]
            self.work += [(call, which, upper) for which, upper in quarters]
        self.spare = 2 * len(self.calls) * slices * slices
        self.total = self.spare + -(-2 * count // (2 * slices)) * 2 * slices
        self.right = self.messages(lambda i, j: max(i, j))
        self.left = self.messages(lambda i, j: slices - 1 - min(i, j))
        self.steps = 0
        for index in range(2 * (len(self.right) + len(self.left)) + 4 * slices):
            if self.senders(self.right, index) or self.senders(self.left, index):
                self.steps = index + 1

    def squares(self, h, i, k, j):
        at = 2 * self.pair_at[h, i, k, j]
        return (at, at) if (h, i) == (k, j) else (at, at + 1)

    def messages(self, reach):
        slices = self.slices
        queues, last = [[] for _ in self.calls], []
        for (h, i, k, j) in self.pair_at:
            far = reach(i, j)
            if far:
                late = self.late(i, j) and self.late(j, i)
                for square in sorted(set(self.squares(h, i, k, j))):
                    if far == 1:
                        late = self.only_last(h, i, k, j)
                    order = (-far, late, self.work_of(h, i, k, j))
                    if far > 1 and h == k:
                        order = (order[2],) + order[:2]
                    elif far > 1:
                        first = self.work_of(self.calls[-1][0], slices - 1, self.calls[-1][1], 0)
                        if far == slices - 1:
                            after = late and self.ends_last(h, i, k, j, reach)
                            order = (2 if late else 0, after, order[2])
                        elif order[2] == first and not late:
                            order = (1, False, order[2])
                        else:
                            order = (2 + slices - far, late, order[2])
                    entry = order + (far, square)
                    (queues[self.calls.index((h, k))] if far > 1 else last).append(entry)
        if self.slices == 2:
            queues, last = [last], []
        found = []
        for queue in [sorted(q) for q in queues] + [sorted(last)]:
            for at in range(0, len(queue), self.count):
                some = queue[at : at + self.count]
                ids = [entry[-1] for entry in some]
                found.append((ids, max(entry[-2] for entry in some)))
        return found

    def late(self, z, j):
        return (2 * z < self.slices) == (2 * j < self.slices)

    def only_last(self, h, i, k, j):
        near = (1, self.slices - 2)
        touched = [part for part, z in ((h, i), (k, j)) if z in near]
        return all(part == self.parts - 1 for part in touched)

    def ends_last(self, h, i, k, j, reach):
        end = self.slices - 1 if reach(self.slices - 1, 0) > reach(0, 0) else 0
        touched = [part for part, z in ((h, i), (k, j)) if z == end]
        return all(part == self.parts - 1 for part in touched)

    def first_ready(self):
        ready = 0
        ids, _ = self.outputs()
        for z in range(self.slices):
            for messages, place in ((self.right, z), (self.left, self.slices - 1 - z)):
                if place == 0:
                    continue
                for k, (squares, _) in enumerate(messages):
                    for j in range(self.slices):
                        parts = self.parts - 1 if self.late(z, j) else self.parts
                        if set(ids[z, :parts, j].ravel()) & set(squares):
                            ready = max(ready, k + 2 * place)
        return ready

    def senders(self, messages, step):
        places = []
        for place in range(self.slices - 1):
            k = step - 2 * place
            if 0 <= k < len(messages) and messages[k][1] > place:
                places.append(place)
        return places

    def table(self):
        rows = np.tile(
            self.spare + np.arange(2 * self.count, dtype=np.int32), (self.slices, self.steps + 2, 1)
        )
        for z in range(self.slices):
            for step in range(self.steps + 2):
                for side, (messages, place) in enumerate(
                    ((self.right, z), (self.left, self.slices - 1 - z))
                ):
                    k = step - 2 * place
                    if 0 <= k < len(messages):
                        for b, square in enumerate(messages[k][0]):
                            rows[z, step, side * self.count + b] = square
        return rows.reshape(-1)

    def work_of(self, h, i, k, j):
        n = self.slices
        return self.work.index((self.calls.index((h, k)), 2 * j // n, 2 * i // n))

    def last_work(self, step):
        need = 0
        for messages in (self.right, self.left):
            for place in range(self.slices):
                k = step - 2 * place
                if 0 <= k < len(messages):
                    for square in messages[k][0]:
                        for (h, i, c, j), at in self.pair_at.items():
                            if at == square // 2:
                                need = max(need, self.work_of(h, i, c, j))
        return need

    def outputs(self):
        z_n, h_n = self.slices, self.parts
        ids = np.zeros((z_n, h_n, z_n, h_n, 2), np.int32)
        modes = np.zeros((z_n, h_n, z_n, h_n), np.int32)
        for z in range(z_n):
            for h in range(h_n):
                for j in range(z_n):
                    for k in range(h_n):
                        if (h, z, k, j) in self.pair_at:
                            ids[z, h, j, k] = self.squares(h, z, k, j)
                            modes[z, h, j, k] = 2 if (h, z) == (k, j) else 0
                        else:
                            ids[z, h, j, k] = self.squares(k, j, h, z)
                            modes[z, h, j, k] = 1
        return ids, modes


def hop_kernel(receives, sends, held, count, steps, step, tab, place, *refs):
    refs = list(refs)
    partial = refs.pop(0) if sends else None
    came = [refs.pop(0) for _ in range(2 if receives else 0)]
    outs = refs[held:]
    kept = [outs.pop(0) for _ in range(2 if receives else 0)]
    sent = [outs.pop(0) for _ in range(2 if sends else 0)]
    own = outs.pop(0) if sends else None
    sems = outs.pop(0)
    at = (place[0] * steps + step) * 2 * count
    slots = [(side, b) for side in range(2) for b in range(count)]
    loads, stores = [], []
    for side, b in slots:
        square = tab[at + side * count + b]
        if sends:
            loads.append(
                pltpu.make_async_copy(partial.at[square], own.at[side, b], sems.at[0, side, b])
            )
            loads[-1].start()
        if receives:
            stores.append(
                pltpu.make_async_copy(came[side].at[b], kept[side].at[square], sems.at[1, side, b])
            )
            stores[-1].start()
    if sends:
        for load, (side, b) in zip(loads, slots):
            load.wait()
            total = own[side, b]
            if receives:
                total = (total.astype(F32) + came[side][b].astype(F32)).astype(BF16)
            sent[side][b] = total
    for store in stores:
        store.wait()


def hop(table, place, steps, step, count, partial, received, kept, sends, after):
    size = partial.shape[1]
    inside = pl.BlockSpec(memory_space=pltpu.VMEM)
    anywhere = pl.BlockSpec(memory_space=pl.ANY)
    numbers = pl.BlockSpec(memory_space=pltpu.SMEM)
    receives = received is not None
    message = jax.ShapeDtypeStruct((count, size, size), BF16)
    in_specs, operands = [numbers, numbers], [table, place]
    out_specs, out_shape, aliases = [], [], {}
    if sends:
        in_specs += [anywhere]
        operands += [partial]
    if receives:
        aliases = {len(operands) + 2: 0, len(operands) + 3: 1}
        in_specs += [inside, inside, anywhere, anywhere]
        operands += [*received, *kept]
        out_specs += [anywhere, anywhere]
        out_shape += [jax.ShapeDtypeStruct(k.shape, k.dtype) for k in kept]
    in_specs += [anywhere] * len(after)
    operands += after
    scratch = []
    if sends:
        out_specs += [inside, inside]
        out_shape += [message, message]
        scratch = [pltpu.VMEM((2, count, size, size), BF16)]
    found = pl.pallas_call(
        functools.partial(
            hop_kernel, receives, sends, (2 if receives else 0) + len(after), count, steps, step
        ),
        in_specs=in_specs,
        out_specs=out_specs,
        out_shape=out_shape,
        scratch_shapes=scratch + [pltpu.SemaphoreType.DMA((2, 2, count))],
        input_output_aliases=aliases,
        compiler_params=params(46 * 1024 * 1024),
        cost_estimate=pl.CostEstimate(
            flops=4 * count * size * size, bytes_accessed=20 * count * size * size, transcendentals=0
        ),
        name="hop",
    )(*operands)
    if receives:
        kept, found = found[:2], found[2:]
    return kept, (found if sends else None)


def piece(slices, parts, early, z, step):
    high = lax.div(2 * z, jnp.int32(slices))
    if not early:
        return parts - 1, high
    return lax.rem(step, jnp.int32(parts)), jnp.where(step < parts, 1 - high, high)


def rows_kernel(slices, parts, span, part, local, early, tab, mode, place, *refs):
    n = slices // 2 * parts * 2
    own, right, left = refs[:n], refs[n : 2 * n], refs[2 * n : 3 * n]
    tiles = refs[-1].shape[4]
    out_ref = refs[-1].reshape(span * part * 2 * tiles, LANES)
    z = place[0]
    h, half = piece(slices, parts, early, z, pl.program_id(0))
    first = half * (slices // 2)
    has_right, has_left = z > 0, z < slices - 1
    size = span * part

    def total(at):
        r = jnp.where(has_right, right[at][0].astype(F32), 0.0)
        l = jnp.where(has_left, left[at][0].astype(F32), 0.0)
        return own[at][0].astype(F32) + r + l

    for j in range(slices // 2):
        for k in range(parts):
            at = 2 * (j * parts + k)
            kind = mode[((z * parts + h) * slices + first + j) * parts + k]

            def put(ri, value, j=j, k=k):
                for d in range(span):
                    for e in range(span):
                        tile = (d * part * 2 + ri) * tiles + ((j * span + e) * local + k * part) // LANES
                        out_ref[pl.ds(tile, part, stride=2 * tiles), :] = value[
                            d * part : (d + 1) * part, e * part : (e + 1) * part
                        ]

            @pl.when(kind == 0)
            def _():
                put(0, total(at))
                put(1, total(at + 1))

            @pl.when(kind == 1)
            def _():
                put(0, total(at).T)
                put(1, -(total(at + 1).T))

            @pl.when(kind == 2)
            def _():
                direct = total(at)
                mirror = direct.T
                row = lax.broadcasted_iota(jnp.int32, (size, size), 0)
                col = lax.broadcasted_iota(jnp.int32, (size, size), 1)
                put(0, jnp.where(row >= col, direct, mirror))
                put(1, jnp.where(row < col, direct, jnp.where(row == col, 0.0, -mirror)))


def visibility_rows(plan, place, partial, kept, span, part, antennas, out):
    slices, parts = plan.slices, plan.parts
    size = span * part
    local = parts * part
    ids, modes = plan.outputs()
    early = out is None
    per_j = parts * 2
    per_half = slices // 2 * per_j

    def start(s, place):
        h, half = piece(slices, parts, early, place[0], s)
        return 2 * (place[0] * parts + h) + half

    def out_map(s, tab, mode, place):
        h, half = piece(slices, parts, early, place[0], s)
        return 0, h, 0, half, 0, 0

    def spec(at):
        return pl.BlockSpec(
            (1, size, size),
            lambda s, tab, mode, place: (tab[start(s, place) * per_half + at], 0, 0),
        )

    tiles = antennas // 2 // LANES
    again = [] if out is None else [out]
    operands = [partial] * per_half + [kept[0]] * per_half + [kept[1]] * per_half + again
    return pl.pallas_call(
        functools.partial(rows_kernel, slices, parts, span, part, local, early),
        grid_spec=pltpu.PrefetchScalarGridSpec(
            num_scalar_prefetch=3,
            grid=(2 * parts - 1 if early else 1,),
            in_specs=[spec(at) for _ in range(3) for at in range(per_half)]
            + [pl.BlockSpec(memory_space=pl.ANY) for _ in again],
            out_specs=pl.BlockSpec(
                (span, 1, part * 2, 1, tiles, LANES), out_map
            ),
        ),
        out_shape=jax.ShapeDtypeStruct((span, parts, part * 2, 2, tiles, LANES), F32),
        input_output_aliases={} if out is None else {3 + 3 * per_half: 0},
        compiler_params=params(),
        cost_estimate=pl.CostEstimate(
            flops=span * local * antennas * 4,
            bytes_accessed=span * local * antennas * 12,
            transcendentals=0,
        ),
        name="visibility_rows",
    )(jnp.asarray(ids.reshape(-1)), jnp.asarray(modes.reshape(-1)), place, *operands)


def on_device(voltages, filter_taps, antenna_flags):
    taps, length = filter_taps.shape
    channels, slices = lax.axis_size("chan"), lax.axis_size("tm")
    local = voltages.shape[1]
    samples = voltages.shape[2]
    frames = samples // length
    part = 128
    parts = local // part
    span = channels // slices

    head = taps * length
    halos = []
    for h in range(parts):
        tail = voltages[:, h * part : (h + 1) * part, samples - head :]
        halos.append(lax.ppermute(tail, "tm", [(i, i + 1) for i in range(slices - 1)]))
    weights = filterbank_weights(filter_taps, channels)
    scale = antenna_flags.reshape(1, local)

    plan = Plan(slices, parts, 4)
    table = jnp.asarray(plan.table())
    place = lax.axis_index("tm").astype(jnp.int32).reshape(1)
    weight = 1.0 / (frames * slices)
    antennas = channels * local
    spectra, token = [], weights
    for h in range(parts):
        pieces = 2 if h == 0 else 1
        chunk = frames // pieces
        found = []
        for t in reversed(range(pieces)):
            own, token = filterbank(
                voltages, halos[h], weights, scale, length, channels, part, h, t * chunk, chunk, token
            )
            found.insert(
                0, lax.all_to_all(own, "chan", split_axis=0, concat_axis=0, tiled=True)
            )
        spectra.append(found)

    done = []

    def extend(partial, kept, count):
        for _ in range(count):
            call, which, upper = plan.work[len(done)]
            h, k = plan.calls[call]
            made = correlate(
                partial, plan.total, slices, call, spectra[h], spectra[k], span, weight, h == k,
                which, upper,
            )
            partial = made[0]
            if kept is None:
                kept = made[1:]
            done.append(call)
        return partial, kept

    def needed(step):
        must = max(0, plan.last_work(step) + 1 - len(done))
        soon = len(done) < len(plan.work) and len(done) <= plan.last_work(step + 1)
        early = soon and step != 0 and (plan.work[len(done)][0] == 0 or step > 3)
        return max(must, 1 if early else 0)

    partial, kept = None, None
    arrived, out = {}, None
    early = max(plan.first_ready(), plan.steps - 1)
    holds = []
    for step in range(plan.steps + 2):
        partial, kept = extend(partial, kept, needed(step))
        sends = step < plan.steps
        received = arrived.pop(step - 2, None)
        kept, outgoing = hop(
            table, place, plan.steps + 2, step, plan.count, partial, received, kept, sends, holds
        )
        holds = []
        if sends:
            right = [(p, p + 1) for p in plan.senders(plan.right, step)]
            end = slices - 1
            left = [(end - p, end - p - 1) for p in plan.senders(plan.left, step)]
            arrived[step] = [
                lax.ppermute(outgoing[0], "tm", right),
                lax.ppermute(outgoing[1], "tm", left),
            ]
        if step == early:
            out = visibility_rows(plan, place, partial, kept, span, part, antennas, None)
            holds = [out]
    out = visibility_rows(plan, place, partial, kept, span, part, antennas, out)
    return out.reshape(span * local, 2, 1, antennas)


def solution(mesh):
    placed = (P(None, "chan", "tm"), P(), P("chan"))
    return jax.shard_map(
        on_device,
        mesh=mesh,
        in_specs=placed,
        out_specs=P("tm", None, "chan", None),
        check_vma=False,
    )
```
